32 devices in a mesh: row: 4 (over y, x), col: 8 (over z, core).
Axes of the slice: x: 2, y: 2, z: 4, core: 2. Of those that a mesh axis runs over, the one named last changes fastest.
Arguments:
- rhs: float32 [32, 16384], P('row', 'col'), may hold values from -60 to 60
- flex_tiles: float32 [32768, 1024], P('row', 'col'), may hold values from -0.25 to 0.25
- flex_cols: int32 [64, 32], P('row', 'col'), may hold values from 0 to 15, as said below
- stiff_tiles: float32 [32768, 1024], P('row', 'col'), may hold values from -0.25 to 0.25
- stiff_cols: int32 [64, 32], P('row', 'col'), may hold values from 0 to 15, as said below
- deflation: float32 [128, 16384], P('row', 'col'), may hold values from -0.375 to 0.375
- coarse_rows: float32 [1024, 1024], P(('row', 'col')), may hold values from -5 to 5, as said below
- face_rows: int32 [16, 1024], P('row', 'col'), may hold values from 0 to 2047, as said below
- face_len: int32 [4, 32], P('row', 'col'), may hold values from 0 to 128, as said below
Outputs:
- solution: float32 [32, 16384], P('row', 'col')
- residual: float32 [32, 16384], P('row', 'col')
- correction: float32 [32, 16384], P('row', 'col')
The draws below stay inside these ranges and needn't reach their ends.
Inputs may be any that keep to these rules, and one draw needn't show every extreme that they name: `flex_cols`: row b of a subdomain's block list names 4 different block columns, the first being b. `stiff_cols`: row b of a subdomain's block list names 4 different block columns, the first being b. `coarse_rows`: the whole matrix is symmetric. `face_rows`: the four lists of a subdomain name 512 different multipliers of it. `face_len`: the two subdomains of a face give it the same length; faces on the grid's boundary have length 0, inner faces at least 32.
All inputs are finite; a program needn't handle non-finite values.
Results may differ from the reference program's by a relative error of at most 0.0003.
Values sent between devices are 32-bit elements; how exact they have to be, the bound alone decides.
No kernel may reach another device: no remote copies, remote signals or barrier semaphores. Data moves between devices by JAX's collectives and lax.ppermute only.
A program may use at most 64 MiB of HBM per device.

```python
import math
import jax
import jax.numpy as jnp
from jax import lax

M = 2048
TILE = 128
TPR = 4
FACE = 128
DEFL = 32
LOADS = 8
ITERS = 3
NB = 16
GRID_ROWS = 4
GRID_COLS = 8
COARSE = 1024


def draw_rhs(key, part):
    first_key, second_key = jax.random.split(jax.random.fold_in(key, 7), 2)
    shape = (GRID_ROWS, LOADS, GRID_COLS, M)
    how_many = GRID_ROWS * GRID_COLS
    position = (jnp.arange(GRID_ROWS)[:, None] * GRID_COLS + jnp.arange(GRID_COLS)[None, :]).astype(jnp.float32) / (how_many - 1)
    position = position[:, None, :, None]
    column_spread = jnp.exp(jax.random.uniform(second_key, (GRID_ROWS, 1, GRID_COLS, M), jnp.float32, 0.0, 2.302585)) / 3.1623
    base_draw = jnp.clip(jax.random.normal(first_key, shape, jnp.float32), -6.0, 6.0)
    values = base_draw * column_spread * 3.0 ** position
    return values.reshape(GRID_ROWS * LOADS, GRID_COLS * M)


def block_lists(key):
    how_many = GRID_ROWS * GRID_COLS * NB
    subkeys = jax.random.split(key, how_many)
    others = jax.vmap(lambda single: jax.random.permutation(single, NB - 1)[:TPR - 1])(subkeys)
    row_ids = (jnp.arange(how_many, dtype=jnp.int32) % NB)[:, None]
    col_ids = jnp.concatenate([row_ids, (row_ids + 1 + others) % NB], axis=1)
    shaped = col_ids.reshape(GRID_ROWS, GRID_COLS, NB, TPR).transpose(0, 2, 1, 3)
    return shaped.reshape(GRID_ROWS * NB, GRID_COLS * TPR).astype(jnp.int32)


def draw_flex_cols(key, part):
    return block_lists(jax.random.fold_in(key, 11))


def draw_stiff_cols(key, part):
    return block_lists(jax.random.fold_in(key, 13))


def draw_coarse_rows(key, part):
    first_key = jax.random.fold_in(jax.random.fold_in(key, 23), 0)
    raw_draw = jnp.clip(jax.random.normal(first_key, (COARSE, COARSE), jnp.float32), -6.0, 6.0)
    symmetric = (raw_draw + raw_draw.T) * (0.5 / math.sqrt(COARSE)) + jnp.eye(COARSE, dtype=jnp.float32)
    return symmetric


def draw_face_rows(key, part):
    subkeys = jax.random.split(jax.random.fold_in(key, 17), GRID_ROWS * GRID_COLS)
    picked = jax.vmap(lambda single: jax.random.permutation(single, M)[:4 * FACE])(subkeys)
    shaped = picked.reshape(GRID_ROWS, GRID_COLS, 4, FACE).transpose(0, 2, 1, 3)
    return shaped.reshape(GRID_ROWS * 4, GRID_COLS * FACE).astype(jnp.int32)


def draw_face_len(key, part):
    first_key, second_key = jax.random.split(jax.random.fold_in(key, 19))
    across = jax.random.randint(first_key, (GRID_ROWS, GRID_COLS - 1), FACE // 4, FACE + 1, jnp.int32)
    across = across.at[0, 0].set(FACE)
    downward = jax.random.randint(second_key, (GRID_ROWS - 1, GRID_COLS), FACE // 4, FACE + 1, jnp.int32)
    padded_down = jnp.pad(downward, ((1, 1), (0, 0)))
    padded_across = jnp.pad(across, ((0, 0), (1, 1)))
    stacked = jnp.stack([padded_down[:-1], padded_down[1:], padded_across[:, :-1], padded_across[:, 1:]], axis=-1)
    return stacked.reshape(GRID_ROWS, GRID_COLS * 4).astype(jnp.int32)


def block_levels(stream_key, shape, shards, low, high):
    def one(dim, blocks):
        heights = jax.random.uniform(jax.random.fold_in(jax.random.fold_in(stream_key, 6), dim), (blocks,), jnp.float32, low / len(shards), high / len(shards))
        return jnp.repeat(jnp.exp(heights), shape[dim] // blocks).reshape((-1,) + (1,) * (len(shape) - dim - 1))

    factor_of = one(*shards[0])
    for cut in shards[1:]:
        factor_of = factor_of * one(*cut)
    return factor_of


def centred(key, extent, scale, reach, cuts=(), kind=jnp.bfloat16):
    level = block_levels(key, extent, cuts, -0.22, 0.18) if cuts else 1.0
    drawn = jax.random.normal(key, extent, jnp.float32) * scale * level
    return jnp.minimum(jnp.maximum(drawn, -reach), reach).astype(kind)


def setup_inputs(seed: int = 0) -> dict:
    keys = jax.random.split(jax.random.key(seed), 10)
    return {
        "rhs": draw_rhs(jax.random.fold_in(keys[9], 71), 0),
        "flex_tiles": centred(keys[1], (GRID_ROWS * NB * TPR * TILE, GRID_COLS * TILE), (TILE * TPR) ** -0.5, 0.25, ((0, 4), (1, 8)), jnp.float32),
        "flex_cols": draw_flex_cols(jax.random.fold_in(keys[9], 71), 0),
        "stiff_tiles": centred(keys[3], (GRID_ROWS * NB * TPR * TILE, GRID_COLS * TILE), (TILE * TPR) ** -0.5, 0.25, ((0, 4), (1, 8)), jnp.float32),
        "stiff_cols": draw_stiff_cols(jax.random.fold_in(keys[9], 71), 0),
        "deflation": centred(keys[5], (GRID_ROWS * DEFL, GRID_COLS * M), (DEFL * 8) ** -0.5, 0.375, ((0, 4), (1, 8)), jnp.float32),
        "coarse_rows": draw_coarse_rows(jax.random.fold_in(keys[9], 71), 0),
        "face_rows": draw_face_rows(jax.random.fold_in(keys[9], 71), 0),
        "face_len": draw_face_len(jax.random.fold_in(keys[9], 71), 0),
    }


PRECISE = lax.Precision.HIGHEST


def sparse_forward(vector, tile_set, columns):
    load_count = vector.shape[0]
    blocks, per_row = columns.shape
    tile_width = tile_set.shape[-1]
    pieces = vector.reshape(load_count, blocks, tile_width)
    picked = jnp.take(pieces, columns.reshape(-1), axis=1).reshape(load_count, blocks, per_row, tile_width)
    product = jnp.einsum("lbkw,bkwv->lbv", picked, tile_set, precision=PRECISE)
    return product.reshape(load_count, blocks * tile_width)


def sparse_backward(vector, tile_set, columns):
    load_count = vector.shape[0]
    blocks, per_row = columns.shape
    tile_width = tile_set.shape[-1]
    pieces = vector.reshape(load_count, blocks, tile_width)
    product = jnp.einsum("lbv,bkwv->lbkw", pieces, tile_set, precision=PRECISE)
    onehot = (columns[:, :, None] == jnp.arange(blocks, dtype=jnp.int32)[None, None, :]).astype(jnp.float32)
    summed = jnp.einsum("lbkw,bkj->ljw", product, onehot, precision=PRECISE)
    return summed.reshape(load_count, blocks * tile_width)


def local_operator(vector, flex_set, flex_list, stiff_set, stiff_list):
    after_flex = sparse_forward(vector, flex_set, flex_list)
    after_stiff = sparse_forward(after_flex, stiff_set, stiff_list)
    back_stiff = sparse_backward(after_stiff, stiff_set, stiff_list)
    return sparse_backward(back_stiff, flex_set, flex_list)


def take_traces(field, face_index):
    return field[:, face_index]


def add_traces(face_index, jump_values):
    return jnp.zeros((LOADS, M), jnp.float32).at[:, face_index].add(jump_values)


def face_term(fields, face_index, live_len):
    traces = jax.vmap(jax.vmap(take_traces))(fields, face_index)
    zero_row = jnp.zeros_like(traces[:1, :, :, 0])
    from_north = jnp.concatenate([zero_row, traces[:-1, :, :, 1]], axis=0)
    from_south = jnp.concatenate([traces[1:, :, :, 0], zero_row], axis=0)
    zero_col = jnp.zeros_like(traces[:, :1, :, 0])
    from_west = jnp.concatenate([zero_col, traces[:, :-1, :, 3]], axis=1)
    from_east = jnp.concatenate([traces[:, 1:, :, 2], zero_col], axis=1)
    partner = jnp.stack([from_north, from_south, from_west, from_east], axis=3)
    slots = jnp.arange(FACE, dtype=jnp.int32)
    live_mask = (slots[None, None, None, :] < live_len[:, :, :, None]).astype(jnp.float32)
    jump_values = (traces - partner) * live_mask[:, :, None]
    return jax.vmap(jax.vmap(add_traces))(face_index, jump_values)


def reference(rhs, flex_tiles, flex_cols, stiff_tiles, stiff_cols, deflation, coarse_rows, face_rows, face_len):
    flex_whole = flex_tiles.reshape(GRID_ROWS, NB, TPR, TILE, GRID_COLS, TILE)
    stiff_whole = stiff_tiles.reshape(GRID_ROWS, NB, TPR, TILE, GRID_COLS, TILE)
    flex_lists = flex_cols.reshape(GRID_ROWS, NB, GRID_COLS, TPR)
    stiff_lists = stiff_cols.reshape(GRID_ROWS, NB, GRID_COLS, TPR)
    basis = deflation.reshape(GRID_ROWS, DEFL, GRID_COLS, M).transpose(0, 2, 1, 3)
    face_index = face_rows.reshape(GRID_ROWS, 4, GRID_COLS, FACE).transpose(0, 2, 1, 3)
    live_len = face_len.reshape(GRID_ROWS, GRID_COLS, 4)

    def one_local(packed):
        index, field = packed
        sub_row = index // GRID_COLS
        sub_col = index % GRID_COLS

        def pick_tiles(whole):
            row_part = lax.dynamic_index_in_dim(whole, sub_row, 0, False)
            return lax.dynamic_index_in_dim(row_part, sub_col, 3, False)

        def pick_list(whole):
            row_part = lax.dynamic_index_in_dim(whole, sub_row, 0, False)
            return lax.dynamic_index_in_dim(row_part, sub_col, 1, False)

        return local_operator(field, pick_tiles(flex_whole), pick_list(flex_lists),
                              pick_tiles(stiff_whole), pick_list(stiff_lists))

    def operate(fields):
        flat = fields.reshape(GRID_ROWS * GRID_COLS, LOADS, M)
        indices = jnp.arange(GRID_ROWS * GRID_COLS, dtype=jnp.int32)
        local_part = lax.map(one_local, (indices, flat)).reshape(fields.shape)
        return fields + local_part + face_term(fields, face_index, live_len)

    def precondition(fields):
        coefficients = jnp.einsum("rclm,rcdm->lrcd", fields, basis, precision=PRECISE)
        flat = coefficients.reshape(LOADS, COARSE)
        energy = jnp.dot(flat, coarse_rows.T, precision=PRECISE).reshape(LOADS, GRID_ROWS, GRID_COLS, DEFL)
        return fields + jnp.einsum("lrcd,rcdm->rclm", energy, basis, precision=PRECISE)

    def totals(first_field, second_field):
        return jnp.sum(first_field * second_field, axis=(0, 1, 3))

    def spread(values):
        return values[None, None, :, None]

    residual = rhs.reshape(GRID_ROWS, LOADS, GRID_COLS, M).transpose(0, 2, 1, 3)
    solution = jnp.zeros_like(residual)
    correction = precondition(residual)
    direction = correction
    image = operate(direction)
    curvature_sum = totals(direction, image)
    descent_sum = totals(residual, direction)
    for iteration in range(ITERS):
        step_size = descent_sum / curvature_sum
        solution = solution + spread(step_size) * direction
        residual = residual - spread(step_size) * image
        correction = precondition(residual)
        if iteration + 1 < ITERS:
            blend = -totals(correction, image) / curvature_sum
            direction = correction + spread(blend) * direction
            image = operate(direction)
            curvature_sum = totals(direction, image)
            descent_sum = totals(residual, direction)

    def to_global(fields):
        return fields.transpose(0, 2, 1, 3).reshape(GRID_ROWS * LOADS, GRID_COLS * M)

    return to_global(solution), to_global(residual), to_global(correction)
```

```python
import functools
from types import SimpleNamespace

import jax
import jax.numpy as jnp
from jax import lax
from jax.experimental import pallas as pl
from jax.experimental.pallas import tpu as pltpu
from jax.sharding import PartitionSpec as P

ITERS = 3
START, FIRST, MIDDLE, LAST = range(4)
LANE = 128
AXES = ("row", "col")
F32, BF16, I32 = jnp.float32, jnp.bfloat16, jnp.int32
NT = (((1,), (1,)), ((), ()))

SMEM = pl.BlockSpec(memory_space=pltpu.SMEM)
VMEM = pl.BlockSpec(memory_space=pltpu.VMEM)
HBM = pl.BlockSpec(memory_space=pltpu.HBM)


def held(shape, dtype=F32):
    return pltpu.VMEM(shape, dtype)


def in_hbm(*arrays):
    return [pltpu.with_memory_space_constraint(x, pltpu.HBM) for x in arrays]


def call(body, outs, specs, name, scratch=(), out_specs=None):
    return pl.pallas_call(
        body,
        out_shape=outs,
        in_specs=specs,
        out_specs=out_specs or jax.tree.map(lambda _: VMEM, outs),
        scratch_shapes=list(scratch),
        compiler_params=pltpu.CompilerParams(vmem_limit_bytes=32 * 1024 * 1024),
        name=name,
    )


def split(x):
    hi = x.astype(BF16)
    return hi, (x - hi.astype(F32)).astype(BF16)


def stacked(x):
    return jnp.concatenate(split(x), axis=0)


def iota(shape, dim):
    return lax.broadcasted_iota(I32, shape, dim)


def pick_lanes(tiles, index):
    rows = tiles[0].shape[0]
    index = jnp.broadcast_to(index, (rows, LANE))
    block, lane = index // LANE, index % LANE
    out = jnp.zeros((rows, LANE), F32)
    for b, tile in enumerate(tiles):
        out = jnp.where(block == b, jnp.take_along_axis(tile, lane, axis=1), out)
    return out


def tiles_of(x):
    return [x[:, b * LANE : (b + 1) * LANE] for b in range(x.shape[1] // LANE)]


def neighbours(pos, count_rows, count_cols):
    i, j = pos[0], pos[1]
    out = []
    for at, count, low in ((i, count_rows, 0), (j, count_cols, 2)):
        even = at % 2 == 0
        for up in (even, jnp.logical_not(even)):
            other = jnp.where(up, at + 1, at - 1)
            there = jnp.logical_and(other >= 0, other < count)
            other = jnp.clip(other, 0, count - 1)
            device = other * count_cols + j if low == 0 else i * count_cols + other
            out.append((jnp.where(up, low + 1, low), device, there))
    return out


def pack(coefs, dots, place):
    rows, width = coefs.shape[0], LANE // 4
    load, lane = iota((rows, LANE), 0), iota((rows, LANE), 1)
    kept = jnp.where(lane // width == (load + place) % 4, coefs, 0.0)
    low = jnp.sum(jnp.where(load < 4, kept, 0.0), axis=0, keepdims=True)
    high = jnp.sum(jnp.where(load >= 4, kept, 0.0), axis=0, keepdims=True)
    scalars = jnp.zeros((rows, LANE), F32)
    for k, dot in enumerate(dots):
        scalars = jnp.where(lane == load * 16 + k, dot, scalars)
    scalars = jnp.sum(scalars, axis=0, keepdims=True)
    return jnp.concatenate([low, high, scalars, jnp.zeros_like(scalars)], axis=0)


def unpack(slot, count, loads):
    width = LANE // 4
    load, lane = iota((loads, LANE), 0), iota((loads, LANE), 1)
    source = (lane // width - load) % 4
    total = jnp.zeros((4, LANE), F32)
    out = []
    for g in range(count // 4):
        mixed = jnp.zeros((loads, LANE), F32)
        for j in range(4):
            piece = slot(4 * g + j)
            total = total + piece
            mixed = jnp.where(source == j, jnp.where(load < 4, piece[0:1], piece[1:2]), mixed)
        lined = mixed
        for q in range(1, 4):
            lined = jnp.where(load % 4 == q, pltpu.roll(mixed, LANE - q * width, axis=1), lined)
        out.append(lined)
    row = jnp.broadcast_to(total[2:3], (loads, LANE))
    dots = [
        jnp.sum(jnp.where(lane == load * 16 + k, row, 0.0), axis=1, keepdims=True) for k in range(4)
    ]
    return jnp.concatenate(out, axis=1), dots


def coefficients(field, basis):
    out = lax.dot_general(stacked(field), basis[...], NT, preferred_element_type=F32)
    out = out[: field.shape[0]] + out[field.shape[0] :]
    return out + pltpu.roll(out, LANE // 4, axis=1)


def write_slots(slots, packed, traces, sides):
    slots[...] = jnp.zeros_like(slots)
    slots[:, slots.shape[1] - 1] = jnp.broadcast_to(packed[None], (slots.shape[0],) + packed.shape)
    for trace, (_, device, there) in zip(traces, sides):

        @pl.when(there)
        def _():
            slots[device, 0] = trace[0:4]
            slots[device, 1] = trace[4:8]


def lead_kernel(grid, pos, *refs):
    sources, (slots, basis, faces), targets, (lengths, rows, sems) = refs[:5], refs[5:8], refs[8:11], refs[11:]
    copies = []
    for k, (src, dst) in enumerate(zip(sources, targets + (rows, lengths))):
        copies.append(pltpu.make_async_copy(src, dst, sems.at[k]))
        copies[-1].start()
    rhs, deflation, _ = targets
    for copy in copies:
        copy.wait()
    sides = neighbours(pos, *grid)
    hi, lo = split(deflation[...])
    basis[...] = jnp.concatenate([hi, lo, hi, lo], axis=0)
    field = rhs[...]
    coefs = coefficients(field, basis)
    tiles = tiles_of(field)
    traces = []
    lane = iota((1, LANE), 1)
    for g, (face, _, _) in enumerate(sides):
        index = rows[pl.ds(face, 1), :]
        here = iota(lengths.shape, 1) == face
        live = jnp.sum(jnp.where(here, lengths[...], 0), axis=1, keepdims=True)
        faces[g : g + 1, :] = index
        faces[g + 4 : g + 5, :] = jnp.where(lane < live, 1, 0)
        traces.append(pick_lanes(tiles, index))
    packed = pack(coefs, (), (pos[0] * grid[1] + pos[1]) % 4)
    write_slots(slots, packed, traces, sides)


def copies_kernel(deflation, coarse, faces, *outs):
    wide = coarse.shape[1]
    tiles = tiles_of(deflation[...])
    for g, out in enumerate(outs):
        out[:, :wide] = coarse[...]
        out[:, wide:] = pick_lanes(tiles, faces[g : g + 1, :])


def prepare_kernel(coarse, faces, *refs):
    received, (weights, partner_basis, inverse) = refs[:4], refs[4:]
    wide = coarse.shape[1]
    defl = coarse.shape[0]
    weights_own = split(coarse[...])
    partner_basis[...] = jnp.zeros_like(partner_basis)
    for g, ref in enumerate(received):
        for half, part in enumerate(split(ref[:, :wide])):
            weights[half * 256 + g * defl : half * 256 + (g + 1) * defl, :] = part
        for half, part in enumerate(weights_own):
            at = half * 256 + LANE + g * defl
            weights[at : at + defl, :] = part
        for half, part in enumerate(split(ref[:, wide:])):
            at = half * LANE + g * defl
            partner_basis[at : at + defl, g * LANE : (g + 1) * LANE] = part
    columns = [
        jnp.transpose(jnp.broadcast_to(faces[g : g + 1, :].astype(F32), (LANE, LANE)))
        for g in range(4)
    ]
    slot, lane = iota((LANE, LANE), 0), iota((LANE, LANE), 1)
    for b in range(inverse.shape[0]):
        found = jnp.zeros((LANE, LANE), F32)
        here = (lane + b * LANE).astype(F32)
        for g in range(4):
            found = jnp.where(columns[g] == here, (slot + (g * LANE + 1)).astype(F32), found)
        inverse[b : b + 1, :] = jnp.sum(found, axis=0, keepdims=True).astype(I32) - 1


def forward(cols, tiles, src, dst, rows):
    per_row, blocks = cols.shape
    deep = per_row * LANE
    for b in range(blocks):
        lhs = jnp.concatenate([src[cols[k, b]] for k in range(per_row)], axis=1)
        out = jnp.dot(lhs, tiles(b), preferred_element_type=F32)
        out = out[:, :LANE] + out[:, LANE:]
        dst[b] = jnp.concatenate([stacked(out[at : at + n] + out[at + n : at + 2 * n]) for at, n in rows], axis=0)


def backward(cols, tiles, src, total, rows):
    per_row, blocks = cols.shape
    total[...] = jnp.zeros_like(total)
    for b in range(blocks):
        lhs = jnp.concatenate([src[b], src[b]], axis=1)
        out = lax.dot_general(lhs, tiles(b), NT, preferred_element_type=F32)
        out = jnp.concatenate([out[at : at + n] + out[at + n : at + 2 * n] for at, n in rows], axis=0)
        for k in range(per_row):
            total[cols[k, b]] += out[:, k * LANE : (k + 1) * LANE]


def restack(total, dst, rows):
    for b in range(dst.shape[0]):
        whole, parts, at = total[b], [], 0
        for _, n in rows:
            parts.append(stacked(whole[at : at + n]))
            at += n
        dst[b] = jnp.concatenate(parts, axis=0)


PARTS = 4


def block_of(tiles, per_row):
    deep = per_row * LANE
    return lambda b: tiles[b * deep : (b + 1) * deep, :]


def transfer(source, target, sems, parts=1):
    step = source.shape[0] // parts
    copies = []
    for k in range(parts):
        at = pl.ds(k * step, step)
        copies.append(pltpu.make_async_copy(source.at[at], target.at[at], sems.at[k]))
        copies[-1].start()
    return copies


def wait(copies):
    for copy in copies:
        copy.wait()


def first_local_kernel(
    flex_raw, stiff_raw, rhs, deflation, flex_list, stiff_list,
    flex_out, stiff_out, local, local_basis,
    first, second, total, raw_first, raw_second, flex, stiff, flex_cols, stiff_cols, sems,
):
    per_row, blocks = flex_cols.shape
    deep = per_row * LANE
    arriving = (
        transfer(flex_raw, raw_first, sems.at[0], PARTS),
        transfer(stiff_raw, raw_second, sems.at[1], PARTS),
    )
    lists = transfer(flex_list, flex_cols, sems.at[2]) + transfer(stiff_list, stiff_cols, sems.at[3])
    loads, defl = rhs.shape[0], deflation.shape[0]
    rows = ((0, loads), (2 * loads, defl))
    for b in range(blocks):
        at = slice(b * LANE, (b + 1) * LANE)
        first[b] = jnp.concatenate([stacked(rhs[:, at]), stacked(deflation[:, at])], axis=0)

    def convert(raw, out, b):
        hi, lo = split(raw[b * deep : (b + 1) * deep, :])
        out[b * deep : (b + 1) * deep, :LANE] = hi
        out[b * deep : (b + 1) * deep, LANE:] = lo

    def converted(raw, out):
        def tiles(b):
            convert(raw, out, b)
            return block_of(out, per_row)(b)

        return tiles

    wait(lists)
    for copy in arriving[0]:
        copy.wait()
    forward(flex_cols, converted(raw_first, flex), first, second, rows)
    leaving = transfer(flex, flex_out, sems.at[2], PARTS)
    for copy in arriving[1]:
        copy.wait()
    forward(stiff_cols, converted(raw_second, stiff), second, first, rows)
    leaving += transfer(stiff, stiff_out, sems.at[3], PARTS)
    backward(stiff_cols, block_of(stiff, per_row), first, total, rows)
    restack(total, second, rows)
    backward(flex_cols, block_of(flex, per_row), second, total, rows)
    for b in range(blocks):
        at = slice(b * LANE, (b + 1) * LANE)
        local[:, at] = total[b][:loads]
        hi, lo = split(total[b][loads:])
        local_basis[:, at] = jnp.concatenate([hi, lo, hi, lo], axis=0)
    wait(leaving)


def local_kernel(
    flex_held, stiff_held, field, flex_list, stiff_list,
    local, first, second, total, flex, stiff, flex_cols, stiff_cols, sems,
):
    per_row, blocks = flex_cols.shape
    lists = transfer(flex_list, flex_cols, sems.at[2]) + transfer(stiff_list, stiff_cols, sems.at[3])
    arriving = (
        transfer(flex_held, flex, sems.at[0], PARTS),
        transfer(stiff_held, stiff, sems.at[1], PARTS),
    )
    rows = ((0, field.shape[0]),)
    for b in range(blocks):
        first[b] = stacked(field[:, b * LANE : (b + 1) * LANE])
    wait(lists)
    wait(arriving[0])
    forward(flex_cols, block_of(flex, per_row), first, second, rows)
    wait(arriving[1])
    forward(stiff_cols, block_of(stiff, per_row), second, first, rows)
    backward(stiff_cols, block_of(stiff, per_row), first, total, rows)
    restack(total, second, rows)
    backward(flex_cols, block_of(flex, per_row), second, total, rows)
    for b in range(blocks):
        local[:, b * LANE : (b + 1) * LANE] = total[b]


def step_kernel(grid, kind, names, out_names, *refs):
    old = SimpleNamespace(**dict(zip(names, refs)))
    out = SimpleNamespace(**dict(zip(out_names, refs[len(names) :])))
    pos, received = old.pos, old.received
    loads = old.residual.shape[0]
    count = received.shape[0]
    last = received.shape[1] - 1
    sides = neighbours(pos, *grid)

    coefs, dots = unpack(lambda s: received[s, last], count, loads)
    both = lax.dot_general(stacked(coefs), old.weights[...], NT, preferred_element_type=F32)
    both = both[:loads] + both[loads:]
    energy = both[:, :256] + both[:, 256:]

    def partner_traces():
        traces = []
        for _, device, there in sides:
            trace = jnp.concatenate([received[device, 0], received[device, 1]], axis=0)
            traces.append(jnp.where(there, trace, 0.0))
        return jnp.concatenate(traces, axis=1)

    keep = {}
    if kind == START:
        residual, local_residual = old.residual[...], old.local_after[...]
        energy_residual, partner_residual = energy, partner_traces()
    else:
        if kind == FIRST:
            curvature, descent = dots[0], dots[1]
            direction, image, energy_image = old.correction[...], old.after[...], energy
            local_image, partner_image = old.local_after[...], partner_traces()
        else:
            energy_sum, project_sum, cross_sum, old_sum = dots
            before = jnp.max(old.curvature[...], axis=1, keepdims=True)
            blend = -cross_sum / before
            curvature = energy_sum + 2.0 * blend * cross_sum + blend * blend * before
            descent = project_sum + blend * old_sum
            direction = old.correction[...] + blend * old.direction[...]
            image = old.after[...] + blend * old.image[...]
            energy_image = energy + blend * old.energy_image[...]
            if kind == MIDDLE:
                local_image = old.local_after[...] + blend * old.local_image[...]
                partner_image = partner_traces() + blend * old.partner_image[...]
        step = descent / curvature
        residual = old.residual[...] - step * image
        energy_residual = old.energy_residual[...] - step * energy_image
        out.solution[...] = step * direction + (0.0 if kind == FIRST else old.solution[...])
        keep.update(residual=residual, direction=direction, image=image, energy_image=energy_image)
        keep.update(curvature=jnp.broadcast_to(curvature, (loads, LANE)))
        if kind != LAST:
            local_residual = old.local_residual[...] - step * local_image
            partner_residual = old.partner_residual[...] - step * partner_image
            keep.update(local_image=local_image, partner_image=partner_image)
    keep.update(energy_residual=energy_residual)

    own = energy_residual[:, LANE:]
    hi, lo = split(own)
    lane = iota(own.shape, 1)
    lhs = jnp.where(lane < LANE // 2, hi.astype(F32), lo.astype(F32)).astype(BF16)
    correction = residual + jnp.dot(lhs, old.basis[...], preferred_element_type=F32)
    keep.update(correction=correction)
    if kind != LAST:
        local = local_residual + jnp.dot(lhs, old.local_basis[...], preferred_element_type=F32)
        hi, lo = split(energy_residual[:, :LANE])
        pairs = jnp.concatenate(
            [jnp.concatenate([hi, hi], axis=1), jnp.concatenate([lo, lo], axis=1)], axis=0
        )
        other = jnp.dot(pairs, old.partner_basis[...], preferred_element_type=F32)
        partner = partner_residual + other[:loads] + other[loads:]
        faces, inverse = old.faces, old.inverse
        tiles = tiles_of(correction)
        jumps = []
        for g in range(4):
            trace = pick_lanes(tiles, faces[g : g + 1, :])
            jump = trace - partner[:, g * LANE : (g + 1) * LANE]
            jumps.append(jnp.where(faces[g + 4 : g + 5, :] > 0, jump, 0.0))
        pieces = []
        for b in range(len(tiles)):
            code = inverse[b : b + 1, :]
            pieces.append(pick_lanes(jumps, jnp.where(code < 0, 4 * LANE, code)))
        after = correction + local + jnp.concatenate(pieces, axis=1)

        dot = lambda a, b: jnp.sum(a * b, axis=1, keepdims=True)
        sums = [dot(correction, after), dot(residual, correction)]
        if kind != START:
            sums += [dot(correction, image), dot(residual, direction)]
        packed = pack(coefficients(after, old.basis), sums, (pos[0] * grid[1] + pos[1]) % 4)
        traces = []
        if kind != MIDDLE:
            tiles = tiles_of(after)
            traces = [pick_lanes(tiles, faces[g : g + 1, :]) for g in range(4)]
        write_slots(out.slots, packed, traces, sides)
        keep.update(after=after, partner_residual=partner_residual, local_residual=local_residual)
    for k, v in keep.items():
        if hasattr(out, k):
            getattr(out, k)[...] = v


def exchange(slots):
    return lax.all_to_all(slots, AXES, 0, 0)


def pairs_of(count, odd):
    low = [(k, k + 1) for k in range(odd, count - 1, 2)]
    return low + [(b, a) for a, b in low]


def shards(
    grid, rhs, flex_tiles, flex_cols, stiff_tiles, stiff_cols, deflation, coarse_rows, face_rows, face_len
):
    loads, wide = rhs.shape
    defl, coarse = coarse_rows.shape
    blocks, per_row = flex_cols.shape
    count = grid[0] * grid[1]
    pos = jnp.stack([lax.axis_index("row"), lax.axis_index("col")]).astype(I32)
    whole = (loads, wide)
    slots = held((count, 3, 4, LANE))

    slots_now, basis, faces, rhs, deflation, coarse_rows = call(
        functools.partial(lead_kernel, grid),
        (
            slots,
            held((4 * defl, wide), BF16),
            held((8, LANE), I32),
            held(whole),
            held(deflation.shape),
            held(coarse_rows.shape),
        ),
        [SMEM] + [HBM] * 5,
        "lead",
        scratch=(pltpu.VMEM(face_len.shape, I32), pltpu.VMEM(face_rows.shape, I32), pltpu.SemaphoreType.DMA((5,))),
    )(pos, *in_hbm(rhs, deflation, coarse_rows, face_rows, face_len))
    received = exchange(slots_now)

    copies = call(
        copies_kernel,
        (jax.ShapeDtypeStruct((defl, coarse + LANE), F32),) * 4,
        [VMEM, VMEM, VMEM],
        "copies",
    )(deflation, coarse_rows, faces)
    copies = [
        lax.ppermute(c, axis, pairs_of(n, odd))
        for c, (axis, n, odd) in zip(
            copies, (("row", grid[0], 0), ("row", grid[0], 1), ("col", grid[1], 0), ("col", grid[1], 1))
        )
    ]
    lists = in_hbm(flex_cols.T, stiff_cols.T)
    tiles_shape = (flex_tiles.shape[0], 2 * LANE)
    tile_scratch = (
        pltpu.VMEM(tiles_shape, BF16),
        pltpu.VMEM(tiles_shape, BF16),
        pltpu.SMEM((per_row, blocks), I32),
        pltpu.SMEM((per_row, blocks), I32),
        pltpu.SemaphoreType.DMA((4, PARTS)),
    )

    def block_scratch(rows):
        return (
            pltpu.VMEM((blocks, 2 * rows, LANE), BF16),
            pltpu.VMEM((blocks, 2 * rows, LANE), BF16),
            pltpu.VMEM((blocks, rows, LANE), F32),
        )

    flex, stiff, local, local_basis = call(
        first_local_kernel,
        (
            pltpu.HBM(tiles_shape, BF16),
            pltpu.HBM(tiles_shape, BF16),
            held(whole),
            held((4 * defl, wide), BF16),
        ),
        [HBM] * 2 + [VMEM] * 2 + [HBM] * 2,
        "first_local",
        scratch=block_scratch(loads + defl)
        + (pltpu.VMEM(flex_tiles.shape, F32), pltpu.VMEM(stiff_tiles.shape, F32))
        + tile_scratch,
        out_specs=(HBM, HBM, VMEM, VMEM),
    )(
        *in_hbm(flex_tiles, stiff_tiles),
        rhs,
        deflation,
        *lists,
    )
    weights, partner_basis, inverse = call(
        prepare_kernel,
        (held((512, coarse), BF16), held((2 * LANE, 4 * LANE), BF16), held((blocks, LANE), I32)),
        [VMEM] * 6,
        "prepare",
    )(coarse_rows, faces, *copies)

    def apply_local(field):
        return call(
            local_kernel, held(whole), [HBM] * 2 + [VMEM] + [HBM] * 2, "local", block_scratch(loads) + tile_scratch
        )(*in_hbm(flex, stiff), field, *lists)

    state = dict(
        pos=pos,
        received=received,
        weights=weights,
        basis=basis,
        local_basis=local_basis,
        partner_basis=partner_basis,
        faces=faces,
        inverse=inverse,
        residual=rhs,
        local_after=local,
        local_residual=local,
    )
    field, energy, traces = held(whole), held((loads, 256)), held((loads, 4 * LANE))
    result = jax.ShapeDtypeStruct(whole, F32)

    def step(kind, **outs):
        done = call(
            functools.partial(step_kernel, grid, kind, tuple(state), tuple(outs)),
            tuple(outs.values()),
            [SMEM] + [VMEM] * (len(state) - 1),
            f"step{kind}",
        )(*state.values())
        state.update(zip(outs, done))

    step(
        START, slots=slots, correction=field, after=field, energy_residual=energy, partner_residual=traces
    )
    for iteration in range(ITERS):
        state.update(received=exchange(state.pop("slots")))
        if iteration + 1 < ITERS:
            state.update(local_after=apply_local(state["after"]))
        kept = dict(
            solution=field, residual=field, correction=field, direction=field, image=field, after=field,
            energy_residual=energy, energy_image=energy, curvature=held((loads, LANE)), slots=slots,
        )
        more = dict(
            partner_residual=traces, local_residual=field, partner_image=traces, local_image=field
        )
        if iteration + 1 == ITERS:
            step(LAST, solution=result, residual=result, correction=result)
        elif iteration == 0 and ITERS > 2:
            step(FIRST, **kept, **more)
        else:
            kept.update(slots=held((count, 1, 4, LANE)))
            step(MIDDLE, **kept)
    return state["solution"], state["residual"], state["correction"]


def solution(mesh):
    grid = (mesh.shape["row"], mesh.shape["col"])
    return jax.shard_map(
        functools.partial(shards, grid),
        mesh=mesh,
        in_specs=(
            P("row", "col"),
            P("row", "col"),
            P("row", "col"),
            P("row", "col"),
            P("row", "col"),
            P("row", "col"),
            P(("row", "col"), None),
            P("row", "col"),
            P("row", "col"),
        ),
        out_specs=(P("row", "col"), P("row", "col"), P("row", "col")),
        check_vma=False,
    )
```

```python
import functools
from types import SimpleNamespace

import jax
import jax.numpy as jnp
from jax import lax
from jax.experimental import pallas as pl
from jax.experimental.pallas import tpu as pltpu
from jax.sharding import PartitionSpec as P

ITERS = 3
START, FIRST, MIDDLE, LAST = range(4)
LANE = 128
AXES = ("row", "col")
F32, BF16, I32 = jnp.float32, jnp.bfloat16, jnp.int32
NT = (((1,), (1,)), ((), ()))

SMEM = pl.BlockSpec(memory_space=pltpu.SMEM)
VMEM = pl.BlockSpec(memory_space=pltpu.VMEM)
HBM = pl.BlockSpec(memory_space=pltpu.HBM)


def held(shape, dtype=F32):
    return pltpu.VMEM(shape, dtype)


def in_hbm(*arrays):
    return [pltpu.with_memory_space_constraint(x, pltpu.HBM) for x in arrays]


def call(body, outs, specs, name, scratch=(), out_specs=None):
    return pl.pallas_call(
        body,
        out_shape=outs,
        in_specs=specs,
        out_specs=out_specs or jax.tree.map(lambda _: VMEM, outs),
        scratch_shapes=list(scratch),
        compiler_params=pltpu.CompilerParams(vmem_limit_bytes=32 * 1024 * 1024),
        name=name,
    )


def split(x):
    hi = x.astype(BF16)
    return hi, (x - hi.astype(F32)).astype(BF16)


def stacked(x):
    return jnp.concatenate(split(x), axis=0)


def iota(shape, dim):
    return lax.broadcasted_iota(I32, shape, dim)


def pick_lanes(tiles, index):
    rows = tiles[0].shape[0]
    index = jnp.broadcast_to(index, (rows, LANE))
    block, lane = index // LANE, index % LANE
    out = jnp.zeros((rows, LANE), F32)
    for b, tile in enumerate(tiles):
        out = jnp.where(block == b, jnp.take_along_axis(tile, lane, axis=1), out)
    return out


def tiles_of(x):
    return [x[:, b * LANE : (b + 1) * LANE] for b in range(x.shape[1] // LANE)]


def neighbours(pos, count_rows, count_cols):
    i, j = pos[0], pos[1]
    out = []
    for at, count, low in ((i, count_rows, 0), (j, count_cols, 2)):
        even = at % 2 == 0
        for up in (even, jnp.logical_not(even)):
            other = jnp.where(up, at + 1, at - 1)
            there = jnp.logical_and(other >= 0, other < count)
            other = jnp.clip(other, 0, count - 1)
            device = other * count_cols + j if low == 0 else i * count_cols + other
            out.append((jnp.where(up, low + 1, low), device, there))
    return out


def pack(coefs, dots, place):
    rows, width = coefs.shape[0], LANE // 4
    load, lane = iota((rows, LANE), 0), iota((rows, LANE), 1)
    kept = jnp.where(lane // width == (load + place) % 4, coefs, 0.0)
    low = jnp.sum(jnp.where(load < 4, kept, 0.0), axis=0, keepdims=True)
    high = jnp.sum(jnp.where(load >= 4, kept, 0.0), axis=0, keepdims=True)
    scalars = jnp.zeros((rows, LANE), F32)
    for k, dot in enumerate(dots):
        scalars = jnp.where(lane == load * 16 + k, dot, scalars)
    scalars = jnp.sum(scalars, axis=0, keepdims=True)
    return jnp.concatenate([low, high, scalars, jnp.zeros_like(scalars)], axis=0)


def unpack(slot, count, loads):
    width = LANE // 4
    load, lane = iota((loads, LANE), 0), iota((loads, LANE), 1)
    source = (lane // width - load) % 4
    total = jnp.zeros((4, LANE), F32)
    out = []
    for g in range(count // 4):
        mixed = jnp.zeros((loads, LANE), F32)
        for j in range(4):
            piece = slot(4 * g + j)
            total = total + piece
            mixed = jnp.where(source == j, jnp.where(load < 4, piece[0:1], piece[1:2]), mixed)
        lined = mixed
        for q in range(1, 4):
            lined = jnp.where(load % 4 == q, pltpu.roll(mixed, LANE - q * width, axis=1), lined)
        out.append(lined)
    row = jnp.broadcast_to(total[2:3], (loads, LANE))
    dots = [
        jnp.sum(jnp.where(lane == load * 16 + k, row, 0.0), axis=1, keepdims=True) for k in range(4)
    ]
    return jnp.concatenate(out, axis=1), dots


def coefficients(field, basis):
    out = lax.dot_general(stacked(field), basis[...], NT, preferred_element_type=F32)
    out = out[: field.shape[0]] + out[field.shape[0] :]
    out = jnp.concatenate([out, out], axis=1)
    return out + pltpu.roll(out, LANE // 4, axis=1)


def expand(energy, basis):
    loads = energy.shape[0]
    out = jnp.dot(stacked(energy[:, : LANE // 2]), basis[...], preferred_element_type=F32)
    return out[:loads] + out[loads:]


def write_slots(slots, packed, traces, sides):
    slots[...] = jnp.zeros_like(slots)
    slots[:, slots.shape[1] - 1] = jnp.broadcast_to(packed[None], (slots.shape[0],) + packed.shape)
    for trace, (_, device, there) in zip(traces, sides):

        @pl.when(there)
        def _():
            slots[device, 0] = trace[0:4]
            slots[device, 1] = trace[4:8]


def lead_kernel(grid, pos, *refs):
    sources, (slots, basis, faces, trace), targets = refs[:5], refs[5:9], refs[9:12]
    lengths, rows, sems = refs[12:]
    copies = []
    for k, (src, dst) in enumerate(zip(sources, targets + (rows, lengths))):
        copies.append(pltpu.make_async_copy(src, dst, sems.at[k]))
        copies[-1].start()
    rhs, deflation, _ = targets
    for copy in copies:
        copy.wait()
    sides = neighbours(pos, *grid)
    basis[...] = stacked(deflation[...])
    field = rhs[...]
    coefs = coefficients(field, basis)
    tiles = tiles_of(field)
    traces = []
    lane = iota((1, LANE), 1)
    for g, (face, _, _) in enumerate(sides):
        index = rows[pl.ds(face, 1), :]
        here = iota(lengths.shape, 1) == face
        live = jnp.sum(jnp.where(here, lengths[...], 0), axis=1, keepdims=True)
        faces[g : g + 1, :] = index
        faces[g + 4 : g + 5, :] = jnp.where(lane < live, 1, 0)
        traces.append(pick_lanes(tiles, index))
    trace[...] = jnp.concatenate(traces, axis=1)
    packed = pack(coefs, (), (pos[0] * grid[1] + pos[1]) % 4)
    write_slots(slots, packed, traces, sides)


def copies_kernel(deflation, coarse, faces, *refs):
    outs, face_basis = refs[:4], refs[4]
    wide = coarse.shape[1]
    tiles = tiles_of(deflation[...])
    for g, out in enumerate(outs):
        out[:, :wide] = coarse[...]
        at_face = pick_lanes(tiles, faces[g : g + 1, :])
        out[:, wide:] = at_face
        face_basis[:, g * LANE : (g + 1) * LANE] = stacked(at_face)


def prepare_kernel(coarse, faces, *refs):
    received, (weights, partner_basis, inverse) = refs[:4], refs[4:]
    wide = coarse.shape[1]
    defl = coarse.shape[0]
    own = split(coarse[...])
    for k, part in enumerate((own[0], own[0], own[1], own[1])):
        weights[LANE + k * defl : LANE + (k + 1) * defl, :] = part
    partner_basis[...] = jnp.zeros_like(partner_basis)
    for g, ref in enumerate(received):
        for half, part in enumerate(split(ref[:, :wide])):
            at = 2 * half * LANE + g * defl
            weights[at : at + defl, :] = part
        for half, part in enumerate(split(ref[:, wide:])):
            at = half * LANE + g * defl
            partner_basis[at : at + defl, g * LANE : (g + 1) * LANE] = part
    columns = [
        jnp.transpose(jnp.broadcast_to(faces[g : g + 1, :].astype(F32), (LANE, LANE)))
        for g in range(4)
    ]
    slot, lane = iota((LANE, LANE), 0), iota((LANE, LANE), 1)
    for b in range(inverse.shape[0]):
        found = jnp.zeros((LANE, LANE), F32)
        here = (lane + b * LANE).astype(F32)
        for g in range(4):
            found = jnp.where(columns[g] == here, (slot + (g * LANE + 1)).astype(F32), found)
        inverse[b : b + 1, :] = jnp.sum(found, axis=0, keepdims=True).astype(I32) - 1


def forward(cols, tiles, src, dst, rows):
    per_row, blocks = cols.shape
    deep = per_row * LANE
    for b in range(blocks):
        lhs = jnp.concatenate([src[cols[k, b]] for k in range(per_row)], axis=1)
        out = jnp.dot(lhs, tiles(b), preferred_element_type=F32)
        out = out[:, :LANE] + out[:, LANE:]
        dst[b] = jnp.concatenate([stacked(out[at : at + n] + out[at + n : at + 2 * n]) for at, n in rows], axis=0)


def backward(cols, tiles, src, total, rows):
    per_row, blocks = cols.shape
    total[...] = jnp.zeros_like(total)
    for b in range(blocks):
        lhs = jnp.concatenate([src[b], src[b]], axis=1)
        out = lax.dot_general(lhs, tiles(b), NT, preferred_element_type=F32)
        out = jnp.concatenate([out[at : at + n] + out[at + n : at + 2 * n] for at, n in rows], axis=0)
        for k in range(per_row):
            total[cols[k, b]] += out[:, k * LANE : (k + 1) * LANE]


def restack(total, dst, rows):
    for b in range(dst.shape[0]):
        whole, parts, at = total[b], [], 0
        for _, n in rows:
            parts.append(stacked(whole[at : at + n]))
            at += n
        dst[b] = jnp.concatenate(parts, axis=0)


PARTS = 2


def transfer(source, target, sems, parts=1):
    step = source.shape[0] // parts
    copies = []
    for k in range(parts):
        at = pl.ds(k * step, step)
        copies.append(pltpu.make_async_copy(source.at[at], target.at[at], sems.at[k]))
        copies[-1].start()
    return copies


def wait(copies):
    for copy in copies:
        copy.wait()


def joined(after, jumps, inverse):
    pieces = tiles_of(jumps)
    out = []
    for b, tile in enumerate(tiles_of(after)):
        code = inverse[b : b + 1, :]
        out.append(tile + pick_lanes(pieces, jnp.where(code < 0, jumps.shape[1], code)))
    return out


def join_kernel(after, jumps, inverse, out):
    out[...] = jnp.concatenate(joined(after[...], jumps[...], inverse), axis=1)


def apply_tiles(lists, arriving, raw, tiles, cols, spaces, rows):
    first, second, total = spaces
    per_row, blocks = cols[0].shape
    deep = per_row * LANE

    def block(s):
        return lambda b: tiles[s][b * deep : (b + 1) * deep, :]

    def converted(s):
        def get(b):
            if b % (blocks // PARTS) == 0:
                arriving[s][b // (blocks // PARTS)].wait()
            at = slice(b * deep, (b + 1) * deep)
            hi, lo = split(raw[s][at, :])
            tiles[s][at, :LANE] = hi
            tiles[s][at, LANE:] = lo
            return block(s)(b)

        return get

    wait(lists)
    forward(cols[0], converted(0), first, second, rows)
    forward(cols[1], converted(1), second, first, rows)
    backward(cols[1], block(1), first, total, rows)
    restack(total, second, rows)
    backward(cols[0], block(0), second, total, rows)


def begin(sources, lists, raw, cols, sems):
    return (
        transfer(lists[0], cols[0], sems.at[2]) + transfer(lists[1], cols[1], sems.at[3]),
        [transfer(sources[s], raw[s], sems.at[s], PARTS) for s in range(2)],
    )


def first_local_kernel(flex, stiff, flex_list, stiff_list, rhs, deflation, local, local_basis, *scratch):
    spaces, raw, tiles, cols, sems = scratch[:3], scratch[3:5], scratch[5:7], scratch[7:9], scratch[9]
    lists, arriving = begin((flex, stiff), (flex_list, stiff_list), raw, cols, sems)
    first, total = spaces[0], spaces[2]
    loads, defl = rhs.shape[0], deflation.shape[0]
    for b in range(first.shape[0]):
        at = slice(b * LANE, (b + 1) * LANE)
        first[b] = jnp.concatenate([stacked(rhs[:, at]), stacked(deflation[:, at])], axis=0)
    apply_tiles(lists, arriving, raw, tiles, cols, spaces, ((0, loads), (2 * loads, defl)))
    for b in range(first.shape[0]):
        at = slice(b * LANE, (b + 1) * LANE)
        local[:, at] = total[b][:loads]
        local_basis[:, at] = stacked(total[b][loads:])


def local_kernel(
    flex, stiff, flex_list, stiff_list, after, jumps, inverse, out, local, *scratch
):
    spaces, raw, tiles, cols, sems = scratch[:3], scratch[3:5], scratch[5:7], scratch[7:9], scratch[9]
    lists, arriving = begin((flex, stiff), (flex_list, stiff_list), raw, cols, sems)
    first, total = spaces[0], spaces[2]
    for b, tile in enumerate(joined(after[...], jumps[...], inverse)):
        out[:, b * LANE : (b + 1) * LANE] = tile
        first[b] = stacked(tile)
    apply_tiles(lists, arriving, raw, tiles, cols, spaces, ((0, after.shape[0]),))
    for b in range(first.shape[0]):
        local[:, b * LANE : (b + 1) * LANE] = total[b]


def step_kernel(grid, kind, names, out_names, *refs):
    old = SimpleNamespace(**dict(zip(names, refs)))
    out = SimpleNamespace(**dict(zip(out_names, refs[len(names) :])))
    pos, received = old.pos, old.received
    loads = old.residual.shape[0]
    count = received.shape[0]
    last = received.shape[1] - 1
    sides = neighbours(pos, *grid)

    coefs, dots = unpack(lambda s: received[s, last], count, loads)
    both = lax.dot_general(stacked(coefs), old.weights[...], NT, preferred_element_type=F32)
    both = both[:loads] + both[loads:]
    own = both[:, LANE : 2 * LANE]
    energy = jnp.concatenate(
        [both[:, :LANE] + both[:, 2 * LANE :], own + pltpu.roll(own, LANE // 2, axis=1)], axis=1
    )

    def partner_traces():
        traces = []
        for _, device, there in sides:
            trace = jnp.concatenate([received[device, 0], received[device, 1]], axis=0)
            traces.append(jnp.where(there, trace, 0.0))
        return jnp.concatenate(traces, axis=1)

    keep = {}
    if kind == START:
        residual, local_residual = old.residual[...], old.local_after[...]
        energy_residual, partner_residual = energy, partner_traces()
        trace_residual = old.trace_after[...]
    else:
        if kind == FIRST:
            curvature, descent = dots[0], dots[1]
            direction, image, energy_image = old.correction[...], old.after[...], energy
            local_image, partner_image = old.local_after[...], partner_traces()
            trace_image = old.trace_after[...]
        else:
            energy_sum, project_sum, cross_sum, old_sum = dots
            before = jnp.max(old.curvature[...], axis=1, keepdims=True)
            blend = -cross_sum / before
            curvature = energy_sum + 2.0 * blend * cross_sum + blend * blend * before
            descent = project_sum + blend * old_sum
            direction = old.correction[...] + blend * old.direction[...]
            image = old.after[...] + blend * old.image[...]
            energy_image = energy + blend * old.energy_image[...]
            if kind == MIDDLE:
                local_image = old.local_after[...] + blend * old.local_image[...]
                partner_image = partner_traces() + blend * old.partner_image[...]
                trace_image = old.trace_after[...] + blend * old.trace_image[...]
        step = descent / curvature
        residual = old.residual[...] - step * image
        energy_residual = old.energy_residual[...] - step * energy_image
        out.solution[...] = step * direction + (0.0 if kind == FIRST else old.solution[...])
        keep.update(residual=residual, direction=direction, image=image, energy_image=energy_image)
        keep.update(curvature=jnp.broadcast_to(curvature, (loads, LANE)))
        if kind != LAST:
            local_residual = old.local_residual[...] - step * local_image
            partner_residual = old.partner_residual[...] - step * partner_image
            trace_residual = old.trace_residual[...] - step * trace_image
            keep.update(local_image=local_image, partner_image=partner_image, trace_image=trace_image)
    keep.update(energy_residual=energy_residual)

    own = energy_residual[:, LANE:]
    correction = residual + expand(own, old.basis)
    keep.update(correction=correction)
    if kind != LAST:
        local = local_residual + expand(own, old.local_basis)
        hi, lo = split(energy_residual[:, :LANE])
        pairs = jnp.concatenate(
            [jnp.concatenate([hi, hi], axis=1), jnp.concatenate([lo, lo], axis=1)], axis=0
        )
        other = jnp.dot(pairs, old.partner_basis[...], preferred_element_type=F32)
        partner = partner_residual + other[:loads] + other[loads:]
        trace = trace_residual + expand(own, old.face_basis)
        faces = old.faces
        live = jnp.concatenate([faces[g + 4 : g + 5, :] for g in range(4)], axis=1)
        jumps = jnp.where(live > 0, trace - partner, 0.0)
        after = correction + local

        dot = lambda a, b: jnp.sum(a * b, axis=1, keepdims=True)
        sums = [dot(correction, after) + dot(trace, jumps), dot(residual, correction)]
        if kind != START:
            sums += [dot(correction, image), dot(residual, direction)]
        coefs = coefficients(after, old.basis) + coefficients(jumps, old.face_basis)
        packed = pack(coefs, sums, (pos[0] * grid[1] + pos[1]) % 4)
        traces = []
        if kind != MIDDLE:
            tiles = tiles_of(after)
            traces = [pick_lanes(tiles, faces[g : g + 1, :]) for g in range(4)]
            traces = [t + j for t, j in zip(traces, tiles_of(jumps))]
            keep.update(trace_after=jnp.concatenate(traces, axis=1))
        write_slots(out.slots, packed, traces, sides)
        keep.update(after=after, jumps=jumps, trace_residual=trace_residual)
        keep.update(partner_residual=partner_residual, local_residual=local_residual)
    for k, v in keep.items():
        if hasattr(out, k):
            getattr(out, k)[...] = v


def exchange(slots):
    return lax.all_to_all(slots, AXES, 0, 0)


def pairs_of(count, odd):
    low = [(k, k + 1) for k in range(odd, count - 1, 2)]
    return low + [(b, a) for a, b in low]


def shards(
    grid, rhs, flex_tiles, flex_cols, stiff_tiles, stiff_cols, deflation, coarse_rows, face_rows, face_len
):
    loads, wide = rhs.shape
    defl, coarse = coarse_rows.shape
    blocks, per_row = flex_cols.shape
    count = grid[0] * grid[1]
    pos = jnp.stack([lax.axis_index("row"), lax.axis_index("col")]).astype(I32)
    whole = (loads, wide)
    slots = held((count, 3, 4, LANE))

    field, energy, traces = held(whole), held((loads, 256)), held((loads, 4 * LANE))

    slots_now, basis, faces, trace, rhs, deflation, coarse_rows = call(
        functools.partial(lead_kernel, grid),
        (
            slots,
            held((2 * defl, wide), BF16),
            held((8, LANE), I32),
            traces,
            field,
            held(deflation.shape),
            held(coarse_rows.shape),
        ),
        [SMEM] + [HBM] * 5,
        "lead",
        scratch=(pltpu.VMEM(face_len.shape, I32), pltpu.VMEM(face_rows.shape, I32), pltpu.SemaphoreType.DMA((5,))),
    )(pos, *in_hbm(rhs, deflation, coarse_rows, face_rows, face_len))
    received = exchange(slots_now)

    *copies, face_basis = call(
        copies_kernel,
        (jax.ShapeDtypeStruct((defl, coarse + LANE), F32),) * 4 + (held((2 * defl, 4 * LANE), BF16),),
        [VMEM, VMEM, VMEM],
        "copies",
    )(deflation, coarse_rows, faces)
    copies = [
        lax.ppermute(c, axis, pairs_of(n, odd))
        for c, (axis, n, odd) in zip(
            copies, (("row", grid[0], 0), ("row", grid[0], 1), ("col", grid[1], 0), ("col", grid[1], 1))
        )
    ]
    lists = in_hbm(flex_tiles, stiff_tiles, flex_cols.T, stiff_cols.T)

    def scratch(rows):
        return (
            (pltpu.VMEM((blocks, 2 * rows, LANE), BF16),) * 2
            + (pltpu.VMEM((blocks, rows, LANE), F32),)
            + (pltpu.VMEM(flex_tiles.shape, F32),) * 2
            + (pltpu.VMEM((flex_tiles.shape[0], 2 * LANE), BF16),) * 2
            + (pltpu.SMEM((per_row, blocks), I32),) * 2
            + (pltpu.SemaphoreType.DMA((4, PARTS)),)
        )

    local, local_basis = call(
        first_local_kernel,
        (field, held((2 * defl, wide), BF16)),
        [HBM] * 4 + [VMEM] * 2,
        "first_local",
        scratch(loads + defl),
    )(*lists, rhs, deflation)
    weights, partner_basis, inverse = call(
        prepare_kernel,
        (held((3 * LANE, coarse), BF16), held((2 * LANE, 4 * LANE), BF16), held((blocks, LANE), I32)),
        [VMEM] * 6,
        "prepare",
    )(coarse_rows, faces, *copies)

    def apply_local(after, jumps):
        return call(local_kernel, (field, field), [HBM] * 4 + [VMEM] * 3, "local", scratch(loads))(
            *lists, after, jumps, inverse
        )

    def join(after, jumps):
        return call(join_kernel, field, [VMEM] * 3, "join")(after, jumps, inverse)

    state = dict(
        pos=pos,
        received=received,
        weights=weights,
        basis=basis,
        local_basis=local_basis,
        partner_basis=partner_basis,
        faces=faces,
        face_basis=face_basis,
        residual=rhs,
        trace_after=trace,
        local_after=local,
        local_residual=local,
    )
    result = jax.ShapeDtypeStruct(whole, F32)

    def step(kind, **outs):
        done = call(
            functools.partial(step_kernel, grid, kind, tuple(state), tuple(outs)),
            tuple(outs.values()),
            [SMEM] + [VMEM] * (len(state) - 1),
            f"step{kind}",
        )(*state.values())
        state.update(zip(outs, done))

    step(
        START, slots=slots, correction=field, after=field, jumps=traces, energy_residual=energy,
        partner_residual=traces, trace_after=traces, trace_residual=traces,
    )
    for iteration in range(ITERS):
        state.update(received=exchange(state.pop("slots")))
        pair = state["after"], state.pop("jumps")
        if iteration + 1 < ITERS:
            state.update(zip(("after", "local_after"), apply_local(*pair)))
        else:
            state.update(after=join(*pair))
        kept = dict(
            solution=field, residual=field, correction=field, direction=field, image=field, after=field,
            jumps=traces, energy_residual=energy, energy_image=energy, curvature=held((loads, LANE)), slots=slots,
        )
        more = dict(
            partner_residual=traces, local_residual=field, partner_image=traces, local_image=field,
            trace_residual=traces, trace_image=traces, trace_after=traces,
        )
        if iteration + 1 == ITERS:
            step(LAST, solution=result, residual=result, correction=result)
        elif iteration == 0 and ITERS > 2:
            step(FIRST, **kept, **more)
        else:
            kept.update(slots=held((count, 1, 4, LANE)))
            step(MIDDLE, **kept)
    return state["solution"], state["residual"], state["correction"]


def solution(mesh):
    grid = (mesh.shape["row"], mesh.shape["col"])
    return jax.shard_map(
        functools.partial(shards, grid),
        mesh=mesh,
        in_specs=(
            P("row", "col"),
            P("row", "col"),
            P("row", "col"),
            P("row", "col"),
            P("row", "col"),
            P("row", "col"),
            P(("row", "col"), None),
            P("row", "col"),
            P("row", "col"),
        ),
        out_specs=(P("row", "col"), P("row", "col"), P("row", "col")),
        check_vma=False,
    )
```

```python
import functools
from types import SimpleNamespace

import jax
import jax.numpy as jnp
from jax import lax
from jax.experimental import pallas as pl
from jax.experimental.pallas import tpu as pltpu
from jax.sharding import PartitionSpec as P

ITERS = 3
START, FIRST, MIDDLE, LAST = range(4)
LANE = 128
AXES = ("row", "col")
F32, BF16, I32 = jnp.float32, jnp.bfloat16, jnp.int32
NT = (((1,), (1,)), ((), ()))

SMEM = pl.BlockSpec(memory_space=pltpu.SMEM)
VMEM = pl.BlockSpec(memory_space=pltpu.VMEM)
HBM = pl.BlockSpec(memory_space=pltpu.HBM)


def held(shape, dtype=F32):
    return pltpu.VMEM(shape, dtype)


def in_hbm(*arrays):
    return [pltpu.with_memory_space_constraint(x, pltpu.HBM) for x in arrays]


def call(body, outs, specs, name, scratch=(), out_specs=None):
    return pl.pallas_call(
        body,
        out_shape=outs,
        in_specs=specs,
        out_specs=out_specs or jax.tree.map(lambda _: VMEM, outs),
        scratch_shapes=list(scratch),
        compiler_params=pltpu.CompilerParams(vmem_limit_bytes=32 * 1024 * 1024),
        name=name,
    )


def split(x):
    hi = x.astype(BF16)
    return hi, (x - hi.astype(F32)).astype(BF16)


def stacked(x):
    return jnp.concatenate(split(x), axis=0)


def iota(shape, dim):
    return lax.broadcasted_iota(I32, shape, dim)


def pick_lanes(tiles, index):
    rows = tiles[0].shape[0]
    index = jnp.broadcast_to(index, (rows, LANE))
    block, lane = index // LANE, index % LANE
    out = jnp.zeros((rows, LANE), F32)
    for b, tile in enumerate(tiles):
        out = jnp.where(block == b, jnp.take_along_axis(tile, lane, axis=1), out)
    return out


def tiles_of(x):
    return [x[:, b * LANE : (b + 1) * LANE] for b in range(x.shape[1] // LANE)]


def neighbours(pos, count_rows, count_cols):
    i, j = pos[0], pos[1]
    out = []
    for at, count, low in ((i, count_rows, 0), (j, count_cols, 2)):
        even = at % 2 == 0
        for up in (even, jnp.logical_not(even)):
            other = jnp.where(up, at + 1, at - 1)
            there = jnp.logical_and(other >= 0, other < count)
            other = jnp.clip(other, 0, count - 1)
            device = other * count_cols + j if low == 0 else i * count_cols + other
            out.append((jnp.where(up, low + 1, low), device, there))
    return out


def pack(coefs, dots, place):
    rows, width = coefs.shape[0], LANE // 4
    load, lane = iota((rows, LANE), 0), iota((rows, LANE), 1)
    kept = jnp.where(lane // width == (load + place) % 4, coefs, 0.0)
    low = jnp.sum(jnp.where(load < 4, kept, 0.0), axis=0, keepdims=True)
    high = jnp.sum(jnp.where(load >= 4, kept, 0.0), axis=0, keepdims=True)
    scalars = jnp.zeros((rows, LANE), F32)
    for k, dot in enumerate(dots):
        scalars = jnp.where(lane == load * 16 + k, dot, scalars)
    scalars = jnp.sum(scalars, axis=0, keepdims=True)
    return jnp.concatenate([low, high, scalars, jnp.zeros_like(scalars)], axis=0)


def unpack(slot, count, loads):
    width = LANE // 4
    load, lane = iota((loads, LANE), 0), iota((loads, LANE), 1)
    source = (lane // width - load) % 4
    total = jnp.zeros((4, LANE), F32)
    out = []
    for g in range(count // 4):
        mixed = jnp.zeros((loads, LANE), F32)
        for j in range(4):
            piece = slot(4 * g + j)
            total = total + piece
            mixed = jnp.where(source == j, jnp.where(load < 4, piece[0:1], piece[1:2]), mixed)
        lined = mixed
        for q in range(1, 4):
            lined = jnp.where(load % 4 == q, pltpu.roll(mixed, LANE - q * width, axis=1), lined)
        out.append(lined)
    row = jnp.broadcast_to(total[2:3], (loads, LANE))
    dots = [
        jnp.sum(jnp.where(lane == load * 16 + k, row, 0.0), axis=1, keepdims=True) for k in range(4)
    ]
    return jnp.concatenate(out, axis=1), dots


def coefficients(field, basis):
    out = lax.dot_general(stacked(field), basis[...], NT, preferred_element_type=F32)
    out = out[: field.shape[0]] + out[field.shape[0] :]
    out = jnp.concatenate([out, out], axis=1)
    return out + pltpu.roll(out, LANE // 4, axis=1)


def expand(energy, basis):
    loads = energy.shape[0]
    out = jnp.dot(stacked(energy[:, : LANE // 2]), basis[...], preferred_element_type=F32)
    return out[:loads] + out[loads:]


def write_slots(slots, packed, traces, sides):
    slots[...] = jnp.zeros_like(slots)
    slots[:, slots.shape[1] - 1] = jnp.broadcast_to(packed[None], (slots.shape[0],) + packed.shape)
    for trace, (_, device, there) in zip(traces, sides):

        @pl.when(there)
        def _():
            slots[device, 0] = trace[0:4]
            slots[device, 1] = trace[4:8]


def lead_kernel(grid, pos, *refs):
    sources, (slots, basis, faces, trace), targets = refs[:5], refs[5:9], refs[9:12]
    lengths, rows, sems = refs[12:]
    copies = []
    for k, (src, dst) in enumerate(zip(sources, targets + (rows, lengths))):
        copies.append(pltpu.make_async_copy(src, dst, sems.at[k]))
        copies[-1].start()
    rhs, deflation, _ = targets
    for copy in copies:
        copy.wait()
    sides = neighbours(pos, *grid)
    basis[...] = stacked(deflation[...])
    field = rhs[...]
    coefs = coefficients(field, basis)
    tiles = tiles_of(field)
    traces = []
    lane = iota((1, LANE), 1)
    for g, (face, _, _) in enumerate(sides):
        index = rows[pl.ds(face, 1), :]
        here = iota(lengths.shape, 1) == face
        live = jnp.sum(jnp.where(here, lengths[...], 0), axis=1, keepdims=True)
        faces[g : g + 1, :] = index
        faces[g + 4 : g + 5, :] = jnp.where(lane < live, 1, 0)
        traces.append(pick_lanes(tiles, index))
    trace[...] = jnp.concatenate(traces, axis=1)
    packed = pack(coefs, (), (pos[0] * grid[1] + pos[1]) % 4)
    write_slots(slots, packed, traces, sides)


def copies_kernel(deflation, coarse, faces, *refs):
    outs, face_basis = refs[:4], refs[4]
    wide = coarse.shape[1]
    tiles = tiles_of(deflation[...])
    for g, out in enumerate(outs):
        out[:, :wide] = coarse[...]
        at_face = pick_lanes(tiles, faces[g : g + 1, :])
        out[:, wide:] = at_face
        face_basis[:, g * LANE : (g + 1) * LANE] = stacked(at_face)


def prepare_kernel(coarse, faces, *refs):
    received, (weights, partner_basis, named) = refs[:4], refs[4:]
    named[...] = find_slots(faces, named.shape[0])
    wide = coarse.shape[1]
    defl = coarse.shape[0]
    own = split(coarse[...])
    for k, part in enumerate((own[0], own[0], own[1], own[1])):
        weights[LANE + k * defl : LANE + (k + 1) * defl, :] = part
    partner_basis[...] = jnp.zeros_like(partner_basis)
    for g, ref in enumerate(received):
        for half, part in enumerate(split(ref[:, :wide])):
            at = 2 * half * LANE + g * defl
            weights[at : at + defl, :] = part
        for half, part in enumerate(split(ref[:, wide:])):
            at = half * LANE + g * defl
            partner_basis[at : at + defl, g * LANE : (g + 1) * LANE] = part


def forward(cols, tiles, src, dst, rows):
    per_row, blocks = cols.shape
    deep = per_row * LANE
    for b in range(blocks):
        lhs = jnp.concatenate([src[cols[k, b]] for k in range(per_row)], axis=1)
        out = jnp.dot(lhs, tiles(b), preferred_element_type=F32)
        out = out[:, :LANE] + out[:, LANE:]
        dst[b] = jnp.concatenate([stacked(out[at : at + n] + out[at + n : at + 2 * n]) for at, n in rows], axis=0)


def backward(cols, tiles, src, total, rows):
    per_row, blocks = cols.shape
    total[...] = jnp.zeros_like(total)
    for b in range(blocks):
        lhs = jnp.concatenate([src[b], src[b]], axis=1)
        out = lax.dot_general(lhs, tiles(b), NT, preferred_element_type=F32)
        out = jnp.concatenate([out[at : at + n] + out[at + n : at + 2 * n] for at, n in rows], axis=0)
        for k in range(per_row):
            total[cols[k, b]] += out[:, k * LANE : (k + 1) * LANE]


def restack(total, dst, rows):
    for b in range(dst.shape[0]):
        whole, parts, at = total[b], [], 0
        for _, n in rows:
            parts.append(stacked(whole[at : at + n]))
            at += n
        dst[b] = jnp.concatenate(parts, axis=0)


def parts_of(blocks):
    return ((0, blocks // 2), (blocks // 2, blocks))


def transfer(source, target, sems, parts=None):
    copies = []
    for k, (low, high) in enumerate(parts or ((0, source.shape[0]),)):
        at = pl.ds(low, high - low)
        copies.append(pltpu.make_async_copy(source.at[at], target.at[at], sems.at[k]))
        copies[-1].start()
    return copies


def wait(copies):
    for copy in copies:
        copy.wait()


def find_slots(faces, blocks):
    lists = faces[0:4, :]
    names = jnp.concatenate([lists[g : g + 1, :] for g in range(4)], axis=1)
    row, slot = iota((blocks, 4 * LANE), 0), iota((blocks, 4 * LANE), 1)
    here = names // LANE == row
    at = jnp.where(here, (slot % LANE).astype(F32), 0.0)
    face = jnp.where(here, (slot // LANE + 1).astype(F32), 0.0)
    lane = iota((LANE, LANE), 1).astype(F32)
    found = []
    for g in range(4):
        column = jnp.transpose(jnp.broadcast_to((lists[g : g + 1, :] % LANE).astype(F32), (LANE, LANE)))
        found.append(jnp.where(column == lane, 1.0, 0.0))
    both = jnp.dot(
        jnp.concatenate([at, face], axis=0).astype(BF16),
        jnp.concatenate(found, axis=0).astype(BF16),
        preferred_element_type=F32,
    )
    at, face = both[:blocks].astype(I32), both[blocks:].astype(I32)
    return jnp.where(face > 0, (face - 1) * LANE + at, 4 * LANE)


def joined(after, jumps, slots):
    pieces = tiles_of(jumps)
    return [
        tile + pick_lanes(pieces, slots[b : b + 1, :]) for b, tile in enumerate(tiles_of(after))
    ]


def apply_tiles(lists, arriving, raw, tiles, cols, spaces, rows):
    first, second, total = spaces
    per_row, blocks = cols[0].shape
    deep = per_row * LANE

    def block(s):
        return lambda b: tiles[s][b * deep : (b + 1) * deep, :]

    def converted(s):
        def get(b):
            for copy, (low, _) in zip(arriving[s], parts_of(blocks)):
                if b == low:
                    copy.wait()
            at = slice(b * deep, (b + 1) * deep)
            hi, lo = split(raw[s][at, :])
            tiles[s][at, :LANE] = hi
            tiles[s][at, LANE:] = lo
            return block(s)(b)

        return get

    wait(lists)
    forward(cols[0], converted(0), first, second, rows)
    forward(cols[1], converted(1), second, first, rows)
    backward(cols[1], block(1), first, total, rows)
    restack(total, second, rows)
    backward(cols[0], block(0), second, total, rows)


def begin(sources, lists, raw, cols, sems):
    per_row, blocks = lists[0].shape
    parts = [(low * per_row * LANE, high * per_row * LANE) for low, high in parts_of(blocks)]
    return (
        transfer(lists[0], cols[0], sems.at[2]) + transfer(lists[1], cols[1], sems.at[3]),
        [transfer(sources[s], raw[s], sems.at[s], parts) for s in range(2)],
    )


def first_local_kernel(flex, stiff, flex_list, stiff_list, rhs, deflation, local, local_basis, *scratch):
    spaces, raw, tiles, cols, sems = scratch[:3], scratch[3:5], scratch[5:7], scratch[7:9], scratch[9]
    lists, arriving = begin((flex, stiff), (flex_list, stiff_list), raw, cols, sems)
    first, total = spaces[0], spaces[2]
    loads, defl = rhs.shape[0], deflation.shape[0]
    for b in range(first.shape[0]):
        at = slice(b * LANE, (b + 1) * LANE)
        first[b] = jnp.concatenate([stacked(rhs[:, at]), stacked(deflation[:, at])], axis=0)
    apply_tiles(lists, arriving, raw, tiles, cols, spaces, ((0, loads), (2 * loads, defl)))
    for b in range(first.shape[0]):
        at = slice(b * LANE, (b + 1) * LANE)
        local[:, at] = total[b][:loads]
        local_basis[:, at] = stacked(total[b][loads:])


def local_kernel(
    flex, stiff, flex_list, stiff_list, after, jumps, named, out, local, *scratch
):
    spaces, raw, tiles, cols, sems = scratch[:3], scratch[3:5], scratch[5:7], scratch[7:9], scratch[9]
    lists, arriving = begin((flex, stiff), (flex_list, stiff_list), raw, cols, sems)
    first, total = spaces[0], spaces[2]
    for b, tile in enumerate(joined(after[...], jumps[...], named)):
        out[:, b * LANE : (b + 1) * LANE] = tile
        first[b] = stacked(tile)
    apply_tiles(lists, arriving, raw, tiles, cols, spaces, ((0, after.shape[0]),))
    for b in range(first.shape[0]):
        local[:, b * LANE : (b + 1) * LANE] = total[b]


def update(dots, curvature):
    energy_sum, project_sum, cross_sum, old_sum = dots
    before = jnp.max(curvature[...], axis=1, keepdims=True)
    blend = -cross_sum / before
    after = energy_sum + 2.0 * blend * cross_sum + blend * blend * before
    return after, project_sum + blend * old_sum, blend


def step_kernel(grid, kind, names, out_names, *refs):
    old = SimpleNamespace(**dict(zip(names, refs)))
    done = len(names) + len(out_names)
    out = SimpleNamespace(**dict(zip(out_names, refs[len(names) : done])))
    pos, received = old.pos, old.received
    loads = old.residual.shape[0]
    count = received.shape[0]
    last = received.shape[1] - 1
    sides = neighbours(pos, *grid)

    coefs, dots = unpack(lambda s: received[s, last], count, loads)
    leaving = []

    def send(k, value, target):
        refs[done + k][...] = value
        leaving.append(pltpu.make_async_copy(refs[done + k], target, refs[-1].at[k]))
        leaving[-1].start()

    if kind == LAST:
        curvature, descent, blend = update(dots, old.curvature)
        step = descent / curvature
        direction = old.correction[...] + blend * old.direction[...]
        send(0, old.solution[...] + step * direction, out.solution)
        residual = old.residual[...] - step * (old.after[...] + blend * old.image[...])
        send(1, residual, out.residual)

    both = lax.dot_general(stacked(coefs), old.weights[...], NT, preferred_element_type=F32)
    both = both[:loads] + both[loads:]
    own = both[:, LANE : 2 * LANE]
    energy = jnp.concatenate(
        [both[:, :LANE] + both[:, 2 * LANE :], own + pltpu.roll(own, LANE // 2, axis=1)], axis=1
    )

    def partner_traces():
        traces = []
        for _, device, there in sides:
            trace = jnp.concatenate([received[device, 0], received[device, 1]], axis=0)
            traces.append(jnp.where(there, trace, 0.0))
        return jnp.concatenate(traces, axis=1)

    if kind == LAST:
        energy = energy[:, LANE:] + blend * old.energy_image[:, LANE:]
        own = old.energy_residual[:, LANE:] - step * energy
        send(2, residual + expand(own, old.basis), out.correction)
        wait(leaving)
        return

    keep = {}
    if kind == START:
        residual, local_residual = old.residual[...], old.local_after[...]
        energy_residual, partner_residual = energy, partner_traces()
        trace_residual = old.trace_after[...]
    else:
        if kind == FIRST:
            curvature, descent = dots[0], dots[1]
            direction, image, energy_image = old.correction[...], old.after[...], energy
            local_image, partner_image = old.local_after[...], partner_traces()
            trace_image = old.trace_after[...]
        else:
            curvature, descent, blend = update(dots, old.curvature)
            direction = old.correction[...] + blend * old.direction[...]
            image = old.after[...] + blend * old.image[...]
            energy_image = energy + blend * old.energy_image[...]
            local_image = old.local_after[...] + blend * old.local_image[...]
            partner_image = partner_traces() + blend * old.partner_image[...]
            trace_image = old.trace_after[...] + blend * old.trace_image[...]
        step = descent / curvature
        residual = old.residual[...] - step * image
        energy_residual = old.energy_residual[...] - step * energy_image
        out.solution[...] = step * direction + (0.0 if kind == FIRST else old.solution[...])
        keep.update(residual=residual, direction=direction, image=image, energy_image=energy_image)
        keep.update(curvature=jnp.broadcast_to(curvature, (loads, LANE)))
        local_residual = old.local_residual[...] - step * local_image
        partner_residual = old.partner_residual[...] - step * partner_image
        trace_residual = old.trace_residual[...] - step * trace_image
        keep.update(local_image=local_image, partner_image=partner_image, trace_image=trace_image)
    keep.update(energy_residual=energy_residual)

    own = energy_residual[:, LANE:]
    hi, lo = split(energy_residual[:, :LANE])
    pairs = jnp.concatenate(
        [jnp.concatenate([hi, hi], axis=1), jnp.concatenate([lo, lo], axis=1)], axis=0
    )
    other = jnp.dot(pairs, old.partner_basis[...], preferred_element_type=F32)
    partner = partner_residual + other[:loads] + other[loads:]
    trace = trace_residual + expand(own, old.face_basis)
    faces = old.faces
    live = jnp.concatenate([faces[g + 4 : g + 5, :] for g in range(4)], axis=1)
    jumps = jnp.where(live > 0, trace - partner, 0.0)
    correction = residual + expand(own, old.basis)
    keep.update(correction=correction)
    local = local_residual + expand(own, old.local_basis)
    after = correction + local

    dot = lambda a, b: jnp.sum(a * b, axis=1, keepdims=True)
    sums = [dot(correction, after) + dot(trace, jumps), dot(residual, correction)]
    if kind != START:
        sums += [dot(correction, image), dot(residual, direction)]
    coefs = coefficients(after, old.basis) + coefficients(jumps, old.face_basis)
    packed = pack(coefs, sums, (pos[0] * grid[1] + pos[1]) % 4)
    traces = []
    if kind != MIDDLE:
        tiles = tiles_of(after)
        traces = [pick_lanes(tiles, faces[g : g + 1, :]) for g in range(4)]
        traces = [t + j for t, j in zip(traces, tiles_of(jumps))]
        keep.update(trace_after=jnp.concatenate(traces, axis=1))
    write_slots(out.slots, packed, traces, sides)
    if kind == MIDDLE:
        after = jnp.concatenate(joined(after, jumps, old.named), axis=1)
    keep.update(after=after, jumps=jumps, trace_residual=trace_residual)
    keep.update(partner_residual=partner_residual, local_residual=local_residual)
    for k, v in keep.items():
        if hasattr(out, k):
            getattr(out, k)[...] = v


def exchange(slots):
    return lax.all_to_all(slots, AXES, 0, 0)


def pairs_of(count, odd):
    low = [(k, k + 1) for k in range(odd, count - 1, 2)]
    return low + [(b, a) for a, b in low]


def shards(
    grid, rhs, flex_tiles, flex_cols, stiff_tiles, stiff_cols, deflation, coarse_rows, face_rows, face_len
):
    loads, wide = rhs.shape
    defl, coarse = coarse_rows.shape
    blocks, per_row = flex_cols.shape
    count = grid[0] * grid[1]
    pos = jnp.stack([lax.axis_index("row"), lax.axis_index("col")]).astype(I32)
    whole = (loads, wide)
    slots = held((count, 3, 4, LANE))

    field, energy, traces = held(whole), held((loads, 256)), held((loads, 4 * LANE))

    slots_now, basis, faces, trace, rhs, deflation, coarse_rows = call(
        functools.partial(lead_kernel, grid),
        (
            slots,
            held((2 * defl, wide), BF16),
            held((8, LANE), I32),
            traces,
            field,
            held(deflation.shape),
            held(coarse_rows.shape),
        ),
        [SMEM] + [HBM] * 5,
        "lead",
        scratch=(pltpu.VMEM(face_len.shape, I32), pltpu.VMEM(face_rows.shape, I32), pltpu.SemaphoreType.DMA((5,))),
    )(pos, *in_hbm(rhs, deflation, coarse_rows, face_rows, face_len))
    received = exchange(slots_now)

    *copies, face_basis = call(
        copies_kernel,
        (jax.ShapeDtypeStruct((defl, coarse + LANE), F32),) * 4 + (held((2 * defl, 4 * LANE), BF16),),
        [VMEM, VMEM, VMEM],
        "copies",
    )(deflation, coarse_rows, faces)
    copies = [
        lax.ppermute(c, axis, pairs_of(n, odd))
        for c, (axis, n, odd) in zip(
            copies, (("row", grid[0], 0), ("row", grid[0], 1), ("col", grid[1], 0), ("col", grid[1], 1))
        )
    ]
    lists = in_hbm(flex_tiles, stiff_tiles, flex_cols.T, stiff_cols.T)

    def scratch(rows):
        return (
            (pltpu.VMEM((blocks, 2 * rows, LANE), BF16),) * 2
            + (pltpu.VMEM((blocks, rows, LANE), F32),)
            + (pltpu.VMEM(flex_tiles.shape, F32),) * 2
            + (pltpu.VMEM((flex_tiles.shape[0], 2 * LANE), BF16),) * 2
            + (pltpu.SMEM((per_row, blocks), I32),) * 2
            + (pltpu.SemaphoreType.DMA((4, 2)),)
        )

    local, local_basis = call(
        first_local_kernel,
        (field, held((2 * defl, wide), BF16)),
        [HBM] * 4 + [VMEM] * 2,
        "first_local",
        scratch(loads + defl),
    )(*lists, rhs, deflation)
    weights, partner_basis, named = call(
        prepare_kernel,
        (held((3 * LANE, coarse), BF16), held((2 * LANE, 4 * LANE), BF16), held((blocks, LANE), I32)),
        [VMEM] * 6,
        "prepare",
    )(coarse_rows, faces, *copies)

    def apply_local(after, jumps):
        return call(local_kernel, (field, field), [HBM] * 4 + [VMEM] * 3, "local", scratch(loads))(
            *lists, after, jumps, named
        )

    state = dict(
        pos=pos,
        received=received,
        weights=weights,
        basis=basis,
        local_basis=local_basis,
        partner_basis=partner_basis,
        faces=faces,
        face_basis=face_basis,
        named=named,
        residual=rhs,
        trace_after=trace,
        local_after=local,
        local_residual=local,
    )
    result = jax.ShapeDtypeStruct(whole, F32)

    def step(kind, **outs):
        last = kind == LAST
        done = call(
            functools.partial(step_kernel, grid, kind, tuple(state), tuple(outs)),
            tuple(outs.values()),
            [SMEM] + [VMEM] * (len(state) - 1),
            f"step{kind}",
            (pltpu.VMEM(whole, F32),) * 3 + (pltpu.SemaphoreType.DMA((3,)),) if last else (),
            (HBM,) * 3 if last else None,
        )(*state.values())
        state.update(zip(outs, done))

    step(
        START, slots=slots, correction=field, after=field, jumps=traces, energy_residual=energy,
        partner_residual=traces, trace_after=traces, trace_residual=traces,
    )
    for iteration in range(ITERS):
        state.update(received=exchange(state.pop("slots")))
        if iteration + 1 < ITERS:
            pair = apply_local(state["after"], state.pop("jumps"))
            state.update(zip(("after", "local_after"), pair))
        kept = dict(
            solution=field, residual=field, correction=field, direction=field, image=field, after=field,
            jumps=traces, energy_residual=energy, energy_image=energy, curvature=held((loads, LANE)), slots=slots,
        )
        more = dict(
            partner_residual=traces, local_residual=field, partner_image=traces, local_image=field,
            trace_residual=traces, trace_image=traces, trace_after=traces,
        )
        if iteration + 1 == ITERS:
            step(LAST, solution=result, residual=result, correction=result)
        elif iteration == 0 and ITERS > 2:
            step(FIRST, **kept, **more)
        else:
            kept.update(slots=held((count, 1, 4, LANE)))
            kept.pop("jumps")
            step(MIDDLE, **kept)
    return state["solution"], state["residual"], state["correction"]


def solution(mesh):
    grid = (mesh.shape["row"], mesh.shape["col"])
    return jax.shard_map(
        functools.partial(shards, grid),
        mesh=mesh,
        in_specs=(
            P("row", "col"),
            P("row", "col"),
            P("row", "col"),
            P("row", "col"),
            P("row", "col"),
            P("row", "col"),
            P(("row", "col"), None),
            P("row", "col"),
            P("row", "col"),
        ),
        out_specs=(P("row", "col"), P("row", "col"), P("row", "col")),
        check_vma=False,
    )
```

```python
import functools
from types import SimpleNamespace

import jax
import jax.numpy as jnp
from jax import lax
from jax.experimental import pallas as pl
from jax.experimental.pallas import tpu as pltpu
from jax.sharding import PartitionSpec as P

ITERS = 3
START, FIRST, MIDDLE, LAST = range(4)
LANE = 128
KEPT = 8
AXES = ("row", "col")
F32, BF16, I32 = jnp.float32, jnp.bfloat16, jnp.int32
NT = (((1,), (1,)), ((), ()))

SMEM = pl.BlockSpec(memory_space=pltpu.SMEM)
VMEM = pl.BlockSpec(memory_space=pltpu.VMEM)
HBM = pl.BlockSpec(memory_space=pltpu.HBM)


def held(shape, dtype=F32):
    return pltpu.VMEM(shape, dtype)


def in_hbm(*arrays):
    return [pltpu.with_memory_space_constraint(x, pltpu.HBM) for x in arrays]


def call(body, outs, specs, name, scratch=(), out_specs=None):
    return pl.pallas_call(
        body,
        out_shape=outs,
        in_specs=specs,
        out_specs=out_specs or jax.tree.map(lambda _: VMEM, outs),
        scratch_shapes=list(scratch),
        compiler_params=pltpu.CompilerParams(vmem_limit_bytes=32 * 1024 * 1024),
        name=name,
    )


def split(x):
    hi = x.astype(BF16)
    return hi, (x - hi.astype(F32)).astype(BF16)


def stacked(x):
    return jnp.concatenate(split(x), axis=0)


def iota(shape, dim):
    return lax.broadcasted_iota(I32, shape, dim)


def pick_lanes(tiles, index):
    rows = tiles[0].shape[0]
    index = jnp.broadcast_to(index, (rows, LANE))
    block, lane = index // LANE, index % LANE
    out = jnp.zeros((rows, LANE), F32)
    for b, tile in enumerate(tiles):
        out = jnp.where(block == b, jnp.take_along_axis(tile, lane, axis=1), out)
    return out


def tiles_of(x):
    return [x[:, b * LANE : (b + 1) * LANE] for b in range(x.shape[1] // LANE)]


def neighbours(pos, count_rows, count_cols):
    i, j = pos[0], pos[1]
    out = []
    for at, count, low in ((i, count_rows, 0), (j, count_cols, 2)):
        even = at % 2 == 0
        for up in (even, jnp.logical_not(even)):
            other = jnp.where(up, at + 1, at - 1)
            there = jnp.logical_and(other >= 0, other < count)
            other = jnp.clip(other, 0, count - 1)
            device = other * count_cols + j if low == 0 else i * count_cols + other
            out.append((jnp.where(up, low + 1, low), device, there))
    return out


def pack(coefs, dots, place):
    rows, width = coefs.shape[0], LANE // 4
    load, lane = iota((rows, LANE), 0), iota((rows, LANE), 1)
    kept = jnp.where(lane // width == (load + place) % 4, coefs, 0.0)
    low = jnp.sum(jnp.where(load < 4, kept, 0.0), axis=0, keepdims=True)
    high = jnp.sum(jnp.where(load >= 4, kept, 0.0), axis=0, keepdims=True)
    scalars = jnp.zeros((rows, LANE), F32)
    for k, dot in enumerate(dots):
        scalars = jnp.where(lane == load * 16 + k, dot, scalars)
    scalars = jnp.sum(scalars, axis=0, keepdims=True)
    return jnp.concatenate([low, high, scalars, jnp.zeros_like(scalars)], axis=0)


def unpack(slot, count, loads):
    width = LANE // 4
    load, lane = iota((loads, LANE), 0), iota((loads, LANE), 1)
    source = (lane // width - load) % 4
    total = jnp.zeros((4, LANE), F32)
    out = []
    for g in range(count // 4):
        mixed = jnp.zeros((loads, LANE), F32)
        for j in range(4):
            piece = slot(4 * g + j)
            total = total + piece
            mixed = jnp.where(source == j, jnp.where(load < 4, piece[0:1], piece[1:2]), mixed)
        lined = mixed
        for q in range(1, 4):
            lined = jnp.where(load % 4 == q, pltpu.roll(mixed, LANE - q * width, axis=1), lined)
        out.append(lined)
    row = jnp.broadcast_to(total[2:3], (loads, LANE))
    dots = [
        jnp.sum(jnp.where(lane == load * 16 + k, row, 0.0), axis=1, keepdims=True) for k in range(4)
    ]
    return jnp.concatenate(out, axis=1), dots


def coefficients(field, basis):
    out = lax.dot_general(stacked(field), basis[...], NT, preferred_element_type=F32)
    out = out[: field.shape[0]] + out[field.shape[0] :]
    out = jnp.concatenate([out, out], axis=1)
    return out + pltpu.roll(out, LANE // 4, axis=1)


def expand(energy, basis):
    loads = energy.shape[0]
    out = jnp.dot(stacked(energy[:, : LANE // 2]), basis[...], preferred_element_type=F32)
    return out[:loads] + out[loads:]


def write_slots(slots, packed, traces, sides):
    slots[...] = jnp.zeros_like(slots)
    slots[:, slots.shape[1] - 1] = jnp.broadcast_to(packed[None], (slots.shape[0],) + packed.shape)
    for trace, (_, device, there) in zip(traces, sides):

        @pl.when(there)
        def _():
            slots[device, 0] = trace[0:4]
            slots[device, 1] = trace[4:8]


def lead_kernel(grid, pos, *refs):
    sources, (slots, basis, faces, trace), targets = refs[:5], refs[5:9], refs[9:12]
    lengths, rows, sems = refs[12:]
    copies = []
    for k, (src, dst) in enumerate(zip(sources, targets + (rows, lengths))):
        copies.append(pltpu.make_async_copy(src, dst, sems.at[k]))
        copies[-1].start()
    rhs, deflation, _ = targets
    for copy in copies:
        copy.wait()
    sides = neighbours(pos, *grid)
    basis[...] = stacked(deflation[...])
    field = rhs[...]
    coefs = coefficients(field, basis)
    tiles = tiles_of(field)
    traces = []
    lane = iota((1, LANE), 1)
    for g, (face, _, _) in enumerate(sides):
        index = rows[pl.ds(face, 1), :]
        here = iota(lengths.shape, 1) == face
        live = jnp.sum(jnp.where(here, lengths[...], 0), axis=1, keepdims=True)
        faces[g : g + 1, :] = index
        faces[g + 4 : g + 5, :] = jnp.where(lane < live, 1, 0)
        traces.append(pick_lanes(tiles, index))
    trace[...] = jnp.concatenate(traces, axis=1)
    packed = pack(coefs, (), (pos[0] * grid[1] + pos[1]) % 4)
    write_slots(slots, packed, traces, sides)


def copies_kernel(deflation, coarse, faces, *refs):
    outs, face_basis = refs[:4], refs[4]
    wide = coarse.shape[1]
    tiles = tiles_of(deflation[...])
    for g, out in enumerate(outs):
        out[:, :wide] = coarse[...]
        at_face = pick_lanes(tiles, faces[g : g + 1, :])
        out[:, wide:] = at_face
        face_basis[:, g * LANE : (g + 1) * LANE] = stacked(at_face)


def prepare_kernel(coarse, *refs):
    received, (weights, partner_basis) = refs[:4], refs[4:]
    wide = coarse.shape[1]
    defl = coarse.shape[0]
    own = split(coarse[...])
    for k, part in enumerate((own[0], own[0], own[1], own[1])):
        weights[LANE + k * defl : LANE + (k + 1) * defl, :] = part
    partner_basis[...] = jnp.zeros_like(partner_basis)
    for g, ref in enumerate(received):
        for half, part in enumerate(split(ref[:, :wide])):
            at = 2 * half * LANE + g * defl
            weights[at : at + defl, :] = part
        for half, part in enumerate(split(ref[:, wide:])):
            at = half * LANE + g * defl
            partner_basis[at : at + defl, g * LANE : (g + 1) * LANE] = part


def forward(cols, tiles, src, dst, rows):
    per_row, blocks = cols.shape
    deep = per_row * LANE
    for b in range(blocks):
        lhs = jnp.concatenate([src[cols[k, b]] for k in range(per_row)], axis=1)
        out = jnp.dot(lhs, tiles(b), preferred_element_type=F32)
        out = out[:, :LANE] + out[:, LANE:]
        dst[b] = jnp.concatenate([stacked(out[at : at + n] + out[at + n : at + 2 * n]) for at, n in rows], axis=0)


def backward(cols, tiles, src, total, rows):
    per_row, blocks = cols.shape
    total[...] = jnp.zeros_like(total)
    for b in range(blocks):
        lhs = jnp.concatenate([src[b], src[b]], axis=1)
        out = lax.dot_general(lhs, tiles(b), NT, preferred_element_type=F32)
        out = jnp.concatenate([out[at : at + n] + out[at + n : at + 2 * n] for at, n in rows], axis=0)
        for k in range(per_row):
            total[cols[k, b]] += out[:, k * LANE : (k + 1) * LANE]


def restack(total, dst, rows):
    for b in range(dst.shape[0]):
        whole, parts, at = total[b], [], 0
        for _, n in rows:
            parts.append(stacked(whole[at : at + n]))
            at += n
        dst[b] = jnp.concatenate(parts, axis=0)


def parts_of(blocks, known=0):
    return ((known, blocks // 2), (blocks // 2, blocks))


def transfer(source, target, sems, parts=None):
    copies = []
    for k, (low, high) in enumerate(parts or ((0, source.shape[0]),)):
        at = pl.ds(low, high - low)
        copies.append(pltpu.make_async_copy(source.at[at], target.at[at], sems.at[k]))
        copies[-1].start()
    return copies


def wait(copies):
    for copy in copies:
        copy.wait()


def find_slots(faces, blocks):
    lists = faces[0:4, :]
    names = jnp.concatenate([lists[g : g + 1, :] for g in range(4)], axis=1)
    row, slot = iota((blocks, 4 * LANE), 0), iota((blocks, 4 * LANE), 1)
    here = names // LANE == row
    at = jnp.where(here, (slot % LANE).astype(F32), 0.0)
    face = jnp.where(here, (slot // LANE + 1).astype(F32), 0.0)
    lane = iota((LANE, LANE), 1).astype(F32)
    found = []
    for g in range(4):
        column = jnp.transpose(jnp.broadcast_to((lists[g : g + 1, :] % LANE).astype(F32), (LANE, LANE)))
        found.append(jnp.where(column == lane, 1.0, 0.0))
    both = jnp.dot(
        jnp.concatenate([at, face], axis=0).astype(BF16),
        jnp.concatenate(found, axis=0).astype(BF16),
        preferred_element_type=F32,
    )
    at, face = both[:blocks].astype(I32), both[blocks:].astype(I32)
    return jnp.where(face > 0, (face - 1) * LANE + at, 4 * LANE)


def joined(after, jumps, slots):
    pieces = tiles_of(jumps)
    return [
        tile + pick_lanes(pieces, slots[b : b + 1, :]) for b, tile in enumerate(tiles_of(after))
    ]


def apply_tiles(lists, arriving, raw, tiles, cols, spaces, rows, kept=None):
    first, second, total = spaces
    per_row, blocks = cols[0].shape
    deep = per_row * LANE

    known = kept.shape[0] // deep if kept is not None else 0

    def block(s):
        def get(b):
            source = kept if s == 0 and b < known else tiles[s]
            return source[b * deep : (b + 1) * deep, :]

        return get

    def converted(s):
        def get(b):
            for copy, (low, _) in zip(arriving[s], parts_of(blocks, known if s == 0 else 0)):
                if b == low:
                    copy.wait()
            if s == 1 or b >= known:
                at = slice(b * deep, (b + 1) * deep)
                hi, lo = split(raw[s][at, :])
                tiles[s][at, :LANE] = hi
                tiles[s][at, LANE:] = lo
            return block(s)(b)

        return get

    wait(lists)
    forward(cols[0], converted(0), first, second, rows)
    forward(cols[1], converted(1), second, first, rows)
    backward(cols[1], block(1), first, total, rows)
    restack(total, second, rows)
    backward(cols[0], block(0), second, total, rows)


def begin(sources, lists, raw, cols, sems, known=0):
    per_row, blocks = lists[0].shape
    deep = per_row * LANE
    parts = [
        [(low * deep, high * deep) for low, high in parts_of(blocks, known * (s == 0))]
        for s in range(2)
    ]
    return (
        transfer(lists[0], cols[0], sems.at[2]) + transfer(lists[1], cols[1], sems.at[3]),
        [transfer(sources[s], raw[s], sems.at[s], parts[s]) for s in range(2)],
    )


def first_local_kernel(
    flex, stiff, flex_list, stiff_list, rhs, deflation, faces, local, local_basis, named, kept, *scratch
):
    spaces, raw, tiles, cols, sems = scratch[:3], scratch[3:5], scratch[5:7], scratch[7:9], scratch[9]
    lists, arriving = begin((flex, stiff), (flex_list, stiff_list), raw, cols, sems)
    first, total = spaces[0], spaces[2]
    loads, defl = rhs.shape[0], deflation.shape[0]
    named[...] = find_slots(faces, named.shape[0])
    for b in range(first.shape[0]):
        at = slice(b * LANE, (b + 1) * LANE)
        first[b] = jnp.concatenate([stacked(rhs[:, at]), stacked(deflation[:, at])], axis=0)
    apply_tiles(lists, arriving, raw, tiles, cols, spaces, ((0, loads), (2 * loads, defl)))
    for b in range(first.shape[0]):
        at = slice(b * LANE, (b + 1) * LANE)
        local[:, at] = total[b][:loads]
        local_basis[:, at] = stacked(total[b][loads:])
    kept[...] = tiles[0][: kept.shape[0], :]


def local_kernel(
    flex, stiff, flex_list, stiff_list, after, jumps, named, kept, out, local, *scratch
):
    spaces, raw, tiles, cols, sems = scratch[:3], scratch[3:5], scratch[5:7], scratch[7:9], scratch[9]
    known = named.shape[0] // KEPT
    lists, arriving = begin((flex, stiff), (flex_list, stiff_list), raw, cols, sems, known)
    first, total = spaces[0], spaces[2]
    for b, tile in enumerate(joined(after[...], jumps[...], named)):
        out[:, b * LANE : (b + 1) * LANE] = tile
        first[b] = stacked(tile)
    apply_tiles(lists, arriving, raw, tiles, cols, spaces, ((0, after.shape[0]),), kept)
    for b in range(first.shape[0]):
        local[:, b * LANE : (b + 1) * LANE] = total[b]


def update(dots, curvature):
    energy_sum, project_sum, cross_sum, old_sum = dots
    before = jnp.max(curvature[...], axis=1, keepdims=True)
    blend = -cross_sum / before
    after = energy_sum + 2.0 * blend * cross_sum + blend * blend * before
    return after, project_sum + blend * old_sum, blend


def step_kernel(grid, kind, names, out_names, *refs):
    old = SimpleNamespace(**dict(zip(names, refs)))
    done = len(names) + len(out_names)
    out = SimpleNamespace(**dict(zip(out_names, refs[len(names) : done])))
    pos, received = old.pos, old.received
    loads = old.residual.shape[0]
    count = received.shape[0]
    last = received.shape[1] - 1
    sides = neighbours(pos, *grid)

    coefs, dots = unpack(lambda s: received[s, last], count, loads)
    leaving = []

    def send(k, value, target):
        refs[done + k][...] = value
        leaving.append(pltpu.make_async_copy(refs[done + k], target, refs[-1].at[k]))
        leaving[-1].start()

    if kind == LAST:
        curvature, descent, blend = update(dots, old.curvature)
        step = descent / curvature
        direction = old.correction[...] + blend * old.direction[...]
        send(0, old.solution[...] + step * direction, out.solution)
        residual = old.residual[...] - step * (old.after[...] + blend * old.image[...])
        send(1, residual, out.residual)

    both = lax.dot_general(stacked(coefs), old.weights[...], NT, preferred_element_type=F32)
    both = both[:loads] + both[loads:]
    own = both[:, LANE : 2 * LANE]
    energy = jnp.concatenate(
        [both[:, :LANE] + both[:, 2 * LANE :], own + pltpu.roll(own, LANE // 2, axis=1)], axis=1
    )

    def partner_traces():
        traces = []
        for _, device, there in sides:
            trace = jnp.concatenate([received[device, 0], received[device, 1]], axis=0)
            traces.append(jnp.where(there, trace, 0.0))
        return jnp.concatenate(traces, axis=1)

    if kind == LAST:
        energy = energy[:, LANE:] + blend * old.energy_image[:, LANE:]
        own = old.energy_residual[:, LANE:] - step * energy
        send(2, residual + expand(own, old.basis), out.correction)
        wait(leaving)
        return

    keep = {}
    if kind == START:
        residual, local_residual = old.residual[...], old.local_after[...]
        energy_residual, partner_residual = energy, partner_traces()
        trace_residual = old.trace_after[...]
    else:
        if kind == FIRST:
            curvature, descent = dots[0], dots[1]
            direction, image, energy_image = old.correction[...], old.after[...], energy
            local_image, partner_image = old.local_after[...], partner_traces()
            trace_image = old.trace_after[...]
        else:
            curvature, descent, blend = update(dots, old.curvature)
            direction = old.correction[...] + blend * old.direction[...]
            image = old.after[...] + blend * old.image[...]
            energy_image = energy + blend * old.energy_image[...]
            local_image = old.local_after[...] + blend * old.local_image[...]
            partner_image = partner_traces() + blend * old.partner_image[...]
            trace_image = old.trace_after[...] + blend * old.trace_image[...]
        step = descent / curvature
        residual = old.residual[...] - step * image
        energy_residual = old.energy_residual[...] - step * energy_image
        out.solution[...] = step * direction + (0.0 if kind == FIRST else old.solution[...])
        keep.update(residual=residual, direction=direction, image=image, energy_image=energy_image)
        keep.update(curvature=jnp.broadcast_to(curvature, (loads, LANE)))
        local_residual = old.local_residual[...] - step * local_image
        partner_residual = old.partner_residual[...] - step * partner_image
        trace_residual = old.trace_residual[...] - step * trace_image
        keep.update(local_image=local_image, partner_image=partner_image, trace_image=trace_image)
    keep.update(energy_residual=energy_residual)

    own = energy_residual[:, LANE:]
    hi, lo = split(energy_residual[:, :LANE])
    pairs = jnp.concatenate(
        [jnp.concatenate([hi, hi], axis=1), jnp.concatenate([lo, lo], axis=1)], axis=0
    )
    other = jnp.dot(pairs, old.partner_basis[...], preferred_element_type=F32)
    partner = partner_residual + other[:loads] + other[loads:]
    trace = trace_residual + expand(own, old.face_basis)
    faces = old.faces
    live = jnp.concatenate([faces[g + 4 : g + 5, :] for g in range(4)], axis=1)
    jumps = jnp.where(live > 0, trace - partner, 0.0)
    correction = residual + expand(own, old.basis)
    keep.update(correction=correction)
    local = local_residual + expand(own, old.local_basis)
    after = correction + local

    dot = lambda a, b: jnp.sum(a * b, axis=1, keepdims=True)
    sums = [dot(correction, after) + dot(trace, jumps), dot(residual, correction)]
    if kind != START:
        sums += [dot(correction, image), dot(residual, direction)]
    coefs = coefficients(after, old.basis) + coefficients(jumps, old.face_basis)
    packed = pack(coefs, sums, (pos[0] * grid[1] + pos[1]) % 4)
    traces = []
    if kind != MIDDLE:
        tiles = tiles_of(after)
        traces = [pick_lanes(tiles, faces[g : g + 1, :]) for g in range(4)]
        traces = [t + j for t, j in zip(traces, tiles_of(jumps))]
        keep.update(trace_after=jnp.concatenate(traces, axis=1))
    write_slots(out.slots, packed, traces, sides)
    if kind == MIDDLE:
        after = jnp.concatenate(joined(after, jumps, old.named), axis=1)
    keep.update(after=after, jumps=jumps, trace_residual=trace_residual)
    keep.update(partner_residual=partner_residual, local_residual=local_residual)
    for k, v in keep.items():
        if hasattr(out, k):
            getattr(out, k)[...] = v


def exchange(slots):
    return lax.all_to_all(slots, AXES, 0, 0)


def pairs_of(count, odd):
    low = [(k, k + 1) for k in range(odd, count - 1, 2)]
    return low + [(b, a) for a, b in low]


def shards(
    grid, rhs, flex_tiles, flex_cols, stiff_tiles, stiff_cols, deflation, coarse_rows, face_rows, face_len
):
    loads, wide = rhs.shape
    defl, coarse = coarse_rows.shape
    blocks, per_row = flex_cols.shape
    count = grid[0] * grid[1]
    pos = jnp.stack([lax.axis_index("row"), lax.axis_index("col")]).astype(I32)
    whole = (loads, wide)
    slots = held((count, 3, 4, LANE))

    field, energy, traces = held(whole), held((loads, 256)), held((loads, 4 * LANE))

    slots_now, basis, faces, trace, rhs, deflation, coarse_rows = call(
        functools.partial(lead_kernel, grid),
        (
            slots,
            held((2 * defl, wide), BF16),
            held((8, LANE), I32),
            traces,
            field,
            held(deflation.shape),
            held(coarse_rows.shape),
        ),
        [SMEM] + [HBM] * 5,
        "lead",
        scratch=(pltpu.VMEM(face_len.shape, I32), pltpu.VMEM(face_rows.shape, I32), pltpu.SemaphoreType.DMA((5,))),
    )(pos, *in_hbm(rhs, deflation, coarse_rows, face_rows, face_len))
    received = exchange(slots_now)

    *copies, face_basis = call(
        copies_kernel,
        (jax.ShapeDtypeStruct((defl, coarse + LANE), F32),) * 4 + (held((2 * defl, 4 * LANE), BF16),),
        [VMEM, VMEM, VMEM],
        "copies",
    )(deflation, coarse_rows, faces)
    copies = [
        lax.ppermute(c, axis, pairs_of(n, odd))
        for c, (axis, n, odd) in zip(
            copies, (("row", grid[0], 0), ("row", grid[0], 1), ("col", grid[1], 0), ("col", grid[1], 1))
        )
    ]
    lists = in_hbm(flex_tiles, stiff_tiles, flex_cols.T, stiff_cols.T)

    def scratch(rows):
        return (
            (pltpu.VMEM((blocks, 2 * rows, LANE), BF16),) * 2
            + (pltpu.VMEM((blocks, rows, LANE), F32),)
            + (pltpu.VMEM(flex_tiles.shape, F32),) * 2
            + (pltpu.VMEM((flex_tiles.shape[0], 2 * LANE), BF16),) * 2
            + (pltpu.SMEM((per_row, blocks), I32),) * 2
            + (pltpu.SemaphoreType.DMA((4, 2)),)
        )

    local, local_basis, named, kept_tiles = call(
        first_local_kernel,
        (
            field,
            held((2 * defl, wide), BF16),
            held((blocks, LANE), I32),
            held((blocks // KEPT * per_row * LANE, 2 * LANE), BF16),
        ),
        [HBM] * 4 + [VMEM] * 3,
        "first_local",
        scratch(loads + defl),
    )(*lists, rhs, deflation, faces)
    weights, partner_basis = call(
        prepare_kernel,
        (held((3 * LANE, coarse), BF16), held((2 * LANE, 4 * LANE), BF16)),
        [VMEM] * 5,
        "prepare",
    )(coarse_rows, *copies)

    def apply_local(after, jumps):
        return call(local_kernel, (field, field), [HBM] * 4 + [VMEM] * 4, "local", scratch(loads))(
            *lists, after, jumps, named, kept_tiles
        )

    state = dict(
        pos=pos,
        received=received,
        weights=weights,
        basis=basis,
        local_basis=local_basis,
        partner_basis=partner_basis,
        faces=faces,
        face_basis=face_basis,
        named=named,
        residual=rhs,
        trace_after=trace,
        local_after=local,
        local_residual=local,
    )
    result = jax.ShapeDtypeStruct(whole, F32)

    def step(kind, **outs):
        last = kind == LAST
        done = call(
            functools.partial(step_kernel, grid, kind, tuple(state), tuple(outs)),
            tuple(outs.values()),
            [SMEM] + [VMEM] * (len(state) - 1),
            f"step{kind}",
            (pltpu.VMEM(whole, F32),) * 3 + (pltpu.SemaphoreType.DMA((3,)),) if last else (),
            (HBM,) * 3 if last else None,
        )(*state.values())
        state.update(zip(outs, done))

    step(
        START, slots=slots, correction=field, after=field, jumps=traces, energy_residual=energy,
        partner_residual=traces, trace_after=traces, trace_residual=traces,
    )
    for iteration in range(ITERS):
        state.update(received=exchange(state.pop("slots")))
        if iteration + 1 < ITERS:
            pair = apply_local(state["after"], state.pop("jumps"))
            state.update(zip(("after", "local_after"), pair))
        kept = dict(
            solution=field, residual=field, correction=field, direction=field, image=field, after=field,
            jumps=traces, energy_residual=energy, energy_image=energy, curvature=held((loads, LANE)), slots=slots,
        )
        more = dict(
            partner_residual=traces, local_residual=field, partner_image=traces, local_image=field,
            trace_residual=traces, trace_image=traces, trace_after=traces,
        )
        if iteration + 1 == ITERS:
            step(LAST, solution=result, residual=result, correction=result)
        elif iteration == 0 and ITERS > 2:
            step(FIRST, **kept, **more)
        else:
            kept.update(slots=held((count, 1, 4, LANE)))
            kept.pop("jumps")
            step(MIDDLE, **kept)
    return state["solution"], state["residual"], state["correction"]


def solution(mesh):
    grid = (mesh.shape["row"], mesh.shape["col"])
    return jax.shard_map(
        functools.partial(shards, grid),
        mesh=mesh,
        in_specs=(
            P("row", "col"),
            P("row", "col"),
            P("row", "col"),
            P("row", "col"),
            P("row", "col"),
            P("row", "col"),
            P(("row", "col"), None),
            P("row", "col"),
            P("row", "col"),
        ),
        out_specs=(P("row", "col"), P("row", "col"), P("row", "col")),
        check_vma=False,
    )
```

```python
import functools
from types import SimpleNamespace

import jax
import jax.numpy as jnp
from jax import lax
from jax.experimental import pallas as pl
from jax.experimental.pallas import tpu as pltpu
from jax.sharding import PartitionSpec as P

ITERS = 3
START, FIRST, MIDDLE, LAST = range(4)
LANE = 128
KEPT = 8
AXES = ("row", "col")
F32, BF16, I32 = jnp.float32, jnp.bfloat16, jnp.int32
NT = (((1,), (1,)), ((), ()))

SMEM = pl.BlockSpec(memory_space=pltpu.SMEM)
VMEM = pl.BlockSpec(memory_space=pltpu.VMEM)
HBM = pl.BlockSpec(memory_space=pltpu.HBM)


def held(shape, dtype=F32):
    return pltpu.VMEM(shape, dtype)


def in_hbm(*arrays):
    return [pltpu.with_memory_space_constraint(x, pltpu.HBM) for x in arrays]


def call(body, outs, specs, name, scratch=(), out_specs=None):
    return pl.pallas_call(
        body,
        out_shape=outs,
        in_specs=specs,
        out_specs=out_specs or jax.tree.map(lambda _: VMEM, outs),
        scratch_shapes=list(scratch),
        compiler_params=pltpu.CompilerParams(vmem_limit_bytes=32 * 1024 * 1024),
        name=name,
    )


def split(x):
    hi = x.astype(BF16)
    return hi, (x - hi.astype(F32)).astype(BF16)


def stacked(x):
    return jnp.concatenate(split(x), axis=0)


def iota(shape, dim):
    return lax.broadcasted_iota(I32, shape, dim)


def pick_lanes(tiles, index):
    rows = tiles[0].shape[0]
    index = jnp.broadcast_to(index, (rows, LANE))
    block, lane = index // LANE, index % LANE
    out = jnp.zeros((rows, LANE), F32)
    for b, tile in enumerate(tiles):
        out = jnp.where(block == b, jnp.take_along_axis(tile, lane, axis=1), out)
    return out


def tiles_of(x):
    return [x[:, b * LANE : (b + 1) * LANE] for b in range(x.shape[1] // LANE)]


def neighbours(pos, count_rows, count_cols):
    i, j = pos[0], pos[1]
    out = []
    for at, count, low in ((i, count_rows, 0), (j, count_cols, 2)):
        even = at % 2 == 0
        for up in (even, jnp.logical_not(even)):
            other = jnp.where(up, at + 1, at - 1)
            there = jnp.logical_and(other >= 0, other < count)
            other = jnp.clip(other, 0, count - 1)
            device = other * count_cols + j if low == 0 else i * count_cols + other
            out.append((jnp.where(up, low + 1, low), device, there))
    return out


def pack(coefs, dots, place):
    rows, width = coefs.shape[0], LANE // 4
    load, lane = iota((rows, LANE), 0), iota((rows, LANE), 1)
    kept = jnp.where(lane // width == (load + place) % 4, coefs, 0.0)
    low = jnp.sum(jnp.where(load < 4, kept, 0.0), axis=0, keepdims=True)
    high = jnp.sum(jnp.where(load >= 4, kept, 0.0), axis=0, keepdims=True)
    scalars = jnp.zeros((rows, LANE), F32)
    for k, dot in enumerate(dots):
        scalars = jnp.where(lane == load * 16 + k, dot, scalars)
    scalars = jnp.sum(scalars, axis=0, keepdims=True)
    return jnp.concatenate([low, high, scalars, jnp.zeros_like(scalars)], axis=0)


def unpack(slot, count, loads):
    width = LANE // 4
    load, lane = iota((loads, LANE), 0), iota((loads, LANE), 1)
    source = (lane // width - load) % 4
    total = jnp.zeros((4, LANE), F32)
    out = []
    for g in range(count // 4):
        mixed = jnp.zeros((loads, LANE), F32)
        for j in range(4):
            piece = slot(4 * g + j)
            total = total + piece
            mixed = jnp.where(source == j, jnp.where(load < 4, piece[0:1], piece[1:2]), mixed)
        lined = mixed
        for q in range(1, 4):
            lined = jnp.where(load % 4 == q, pltpu.roll(mixed, LANE - q * width, axis=1), lined)
        out.append(lined)
    row = jnp.broadcast_to(total[2:3], (loads, LANE))
    dots = [
        jnp.sum(jnp.where(lane == load * 16 + k, row, 0.0), axis=1, keepdims=True) for k in range(4)
    ]
    return jnp.concatenate(out, axis=1), dots


def coefficients(field, basis):
    out = lax.dot_general(stacked(field), basis[...], NT, preferred_element_type=F32)
    out = out[: field.shape[0]] + out[field.shape[0] :]
    out = jnp.concatenate([out, out], axis=1)
    return out + pltpu.roll(out, LANE // 4, axis=1)


def expand(energy, basis):
    loads = energy.shape[0]
    out = jnp.dot(stacked(energy[:, : LANE // 2]), basis[...], preferred_element_type=F32)
    return out[:loads] + out[loads:]


def write_slots(slots, packed, traces, sides):
    slots[...] = jnp.zeros_like(slots)
    slots[:, slots.shape[1] - 1] = jnp.broadcast_to(packed[None], (slots.shape[0],) + packed.shape)
    for trace, (_, device, there) in zip(traces, sides):

        @pl.when(there)
        def _():
            slots[device, 0] = trace[0:4]
            slots[device, 1] = trace[4:8]


def lead_kernel(grid, pos, *refs):
    sources, (slots, basis, faces, trace), targets = refs[:5], refs[5:9], refs[9:12]
    lengths, rows, sems = refs[12:]
    copies = []
    for k, (src, dst) in enumerate(zip(sources, targets + (rows, lengths))):
        copies.append(pltpu.make_async_copy(src, dst, sems.at[k]))
        copies[-1].start()
    rhs, deflation, _ = targets
    copies[1].wait()
    sides = neighbours(pos, *grid)
    basis[...] = stacked(deflation[...])
    for k in (0, 3, 4):
        copies[k].wait()
    field = rhs[...]
    coefs = coefficients(field, basis)
    tiles = tiles_of(field)
    traces = []
    lane = iota((1, LANE), 1)
    for g, (face, _, _) in enumerate(sides):
        index = rows[pl.ds(face, 1), :]
        here = iota(lengths.shape, 1) == face
        live = jnp.sum(jnp.where(here, lengths[...], 0), axis=1, keepdims=True)
        faces[g : g + 1, :] = index
        faces[g + 4 : g + 5, :] = jnp.where(lane < live, 1, 0)
        traces.append(pick_lanes(tiles, index))
    trace[...] = jnp.concatenate(traces, axis=1)
    packed = pack(coefs, (), (pos[0] * grid[1] + pos[1]) % 4)
    write_slots(slots, packed, traces, sides)
    copies[2].wait()


def copies_kernel(deflation, coarse, faces, *refs):
    outs, face_basis = refs[:4], refs[4]
    wide = coarse.shape[1]
    tiles = tiles_of(deflation[...])
    for g, out in enumerate(outs):
        out[:, :wide] = coarse[...]
        at_face = pick_lanes(tiles, faces[g : g + 1, :])
        out[:, wide:] = at_face
        face_basis[:, g * LANE : (g + 1) * LANE] = stacked(at_face)


def prepare_kernel(coarse, *refs):
    received, (weights, partner_basis) = refs[:4], refs[4:]
    wide = coarse.shape[1]
    defl = coarse.shape[0]
    own = split(coarse[...])
    for k, part in enumerate((own[0], own[0], own[1], own[1])):
        weights[LANE + k * defl : LANE + (k + 1) * defl, :] = part
    partner_basis[...] = jnp.zeros_like(partner_basis)
    for g, ref in enumerate(received):
        for half, part in enumerate(split(ref[:, :wide])):
            at = 2 * half * LANE + g * defl
            weights[at : at + defl, :] = part
        for half, part in enumerate(split(ref[:, wide:])):
            at = half * LANE + g * defl
            partner_basis[at : at + defl, g * LANE : (g + 1) * LANE] = part


def forward(cols, tiles, src, dst, rows):
    per_row, blocks = cols.shape
    deep = per_row * LANE
    for b in range(blocks):
        lhs = jnp.concatenate([src[cols[k, b]] for k in range(per_row)], axis=1)
        out = jnp.dot(lhs, tiles(b), preferred_element_type=F32)
        out = out[:, :LANE] + out[:, LANE:]
        dst[b] = jnp.concatenate([stacked(out[at : at + n] + out[at + n : at + 2 * n]) for at, n in rows], axis=0)


def backward(cols, tiles, src, total, rows):
    per_row, blocks = cols.shape
    total[...] = jnp.zeros_like(total)
    for b in range(blocks):
        lhs = jnp.concatenate([src[b], src[b]], axis=1)
        out = lax.dot_general(lhs, tiles(b), NT, preferred_element_type=F32)
        out = jnp.concatenate([out[at : at + n] + out[at + n : at + 2 * n] for at, n in rows], axis=0)
        for k in range(per_row):
            total[cols[k, b]] += out[:, k * LANE : (k + 1) * LANE]


def restack(total, dst, rows):
    for b in range(dst.shape[0]):
        whole, parts, at = total[b], [], 0
        for _, n in rows:
            parts.append(stacked(whole[at : at + n]))
            at += n
        dst[b] = jnp.concatenate(parts, axis=0)


def parts_of(blocks, known=0):
    return ((known, blocks // 2), (blocks // 2, blocks))


def transfer(source, target, sems, parts=None):
    copies = []
    for k, (low, high) in enumerate(parts or ((0, source.shape[0]),)):
        at = pl.ds(low, high - low)
        copies.append(pltpu.make_async_copy(source.at[at], target.at[at], sems.at[k]))
        copies[-1].start()
    return copies


def wait(copies):
    for copy in copies:
        copy.wait()


def find_slots(faces, blocks):
    lists = faces[0:4, :]
    names = jnp.concatenate([lists[g : g + 1, :] for g in range(4)], axis=1)
    row, slot = iota((blocks, 4 * LANE), 0), iota((blocks, 4 * LANE), 1)
    here = names // LANE == row
    at = jnp.where(here, (slot % LANE).astype(F32), 0.0)
    face = jnp.where(here, (slot // LANE + 1).astype(F32), 0.0)
    lane = iota((LANE, LANE), 1).astype(F32)
    found = []
    for g in range(4):
        column = jnp.transpose(jnp.broadcast_to((lists[g : g + 1, :] % LANE).astype(F32), (LANE, LANE)))
        found.append(jnp.where(column == lane, 1.0, 0.0))
    both = jnp.dot(
        jnp.concatenate([at, face], axis=0).astype(BF16),
        jnp.concatenate(found, axis=0).astype(BF16),
        preferred_element_type=F32,
    )
    at, face = both[:blocks].astype(I32), both[blocks:].astype(I32)
    return jnp.where(face > 0, (face - 1) * LANE + at, 4 * LANE)


def joined(after, jumps, slots):
    pieces = tiles_of(jumps)
    return [
        tile + pick_lanes(pieces, slots[b : b + 1, :]) for b, tile in enumerate(tiles_of(after))
    ]


def apply_tiles(lists, arriving, raw, tiles, cols, spaces, rows, kept=None):
    first, second, total = spaces
    per_row, blocks = cols[0].shape
    deep = per_row * LANE

    known = kept.shape[0] // deep if kept is not None else 0

    def block(s):
        def get(b):
            source = kept if s == 0 and b < known else tiles[s]
            return source[b * deep : (b + 1) * deep, :]

        return get

    def converted(s):
        def get(b):
            for copy, (low, _) in zip(arriving[s], parts_of(blocks, known if s == 0 else 0)):
                if b == low:
                    copy.wait()
            if s == 1 or b >= known:
                at = slice(b * deep, (b + 1) * deep)
                hi, lo = split(raw[s][at, :])
                tiles[s][at, :LANE] = hi
                tiles[s][at, LANE:] = lo
            return block(s)(b)

        return get

    wait(lists)
    forward(cols[0], converted(0), first, second, rows)
    forward(cols[1], converted(1), second, first, rows)
    backward(cols[1], block(1), first, total, rows)
    restack(total, second, rows)
    backward(cols[0], block(0), second, total, rows)


def begin(sources, lists, raw, cols, sems, known=0):
    per_row, blocks = lists[0].shape
    deep = per_row * LANE
    parts = [
        [(low * deep, high * deep) for low, high in parts_of(blocks, known * (s == 0))]
        for s in range(2)
    ]
    return (
        transfer(lists[0], cols[0], sems.at[2]) + transfer(lists[1], cols[1], sems.at[3]),
        [transfer(sources[s], raw[s], sems.at[s], parts[s]) for s in range(2)],
    )


def first_local_kernel(
    flex, stiff, flex_list, stiff_list, rhs, deflation, faces, local, local_basis, named, kept, *scratch
):
    spaces, raw, tiles, cols, sems = scratch[:3], scratch[3:5], scratch[5:7], scratch[7:9], scratch[9]
    lists, arriving = begin((flex, stiff), (flex_list, stiff_list), raw, cols, sems)
    first, total = spaces[0], spaces[2]
    loads, defl = rhs.shape[0], deflation.shape[0]
    named[...] = find_slots(faces, named.shape[0])
    for b in range(first.shape[0]):
        at = slice(b * LANE, (b + 1) * LANE)
        first[b] = jnp.concatenate([stacked(rhs[:, at]), stacked(deflation[:, at])], axis=0)
    apply_tiles(lists, arriving, raw, tiles, cols, spaces, ((0, loads), (2 * loads, defl)))
    for b in range(first.shape[0]):
        at = slice(b * LANE, (b + 1) * LANE)
        local[:, at] = total[b][:loads]
        local_basis[:, at] = stacked(total[b][loads:])
    kept[...] = tiles[0][: kept.shape[0], :]


def local_kernel(
    flex, stiff, flex_list, stiff_list, after, jumps, named, kept, out, local, *scratch
):
    spaces, raw, tiles, cols, sems = scratch[:3], scratch[3:5], scratch[5:7], scratch[7:9], scratch[9]
    known = named.shape[0] // KEPT
    lists, arriving = begin((flex, stiff), (flex_list, stiff_list), raw, cols, sems, known)
    first, total = spaces[0], spaces[2]
    for b, tile in enumerate(joined(after[...], jumps[...], named)):
        out[:, b * LANE : (b + 1) * LANE] = tile
        first[b] = stacked(tile)
    apply_tiles(lists, arriving, raw, tiles, cols, spaces, ((0, after.shape[0]),), kept)
    for b in range(first.shape[0]):
        local[:, b * LANE : (b + 1) * LANE] = total[b]


def update(dots, curvature):
    energy_sum, project_sum, cross_sum, old_sum = dots
    before = jnp.max(curvature[...], axis=1, keepdims=True)
    blend = -cross_sum / before
    after = energy_sum + 2.0 * blend * cross_sum + blend * blend * before
    return after, project_sum + blend * old_sum, blend


def step_kernel(grid, kind, names, out_names, *refs):
    old = SimpleNamespace(**dict(zip(names, refs)))
    done = len(names) + len(out_names)
    out = SimpleNamespace(**dict(zip(out_names, refs[len(names) : done])))
    pos, received = old.pos, old.received
    loads = old.residual.shape[0]
    count = received.shape[0]
    last = received.shape[1] - 1
    sides = neighbours(pos, *grid)

    coefs, dots = unpack(lambda s: received[s, last], count, loads)
    leaving = []

    def send(k, value, target):
        refs[done + k][...] = value
        leaving.append(pltpu.make_async_copy(refs[done + k], target, refs[-1].at[k]))
        leaving[-1].start()

    if kind == LAST:
        curvature, descent, blend = update(dots, old.curvature)
        step = descent / curvature
        direction = old.correction[...] + blend * old.direction[...]
        send(0, old.solution[...] + step * direction, out.solution)
        residual = old.residual[...] - step * (old.after[...] + blend * old.image[...])
        send(1, residual, out.residual)

    both = lax.dot_general(stacked(coefs), old.weights[...], NT, preferred_element_type=F32)
    both = both[:loads] + both[loads:]
    own = both[:, LANE : 2 * LANE]
    energy = jnp.concatenate(
        [both[:, :LANE] + both[:, 2 * LANE :], own + pltpu.roll(own, LANE // 2, axis=1)], axis=1
    )

    def partner_traces():
        traces = []
        for _, device, there in sides:
            trace = jnp.concatenate([received[device, 0], received[device, 1]], axis=0)
            traces.append(jnp.where(there, trace, 0.0))
        return jnp.concatenate(traces, axis=1)

    if kind == LAST:
        energy = energy[:, LANE:] + blend * old.energy_image[:, LANE:]
        own = old.energy_residual[:, LANE:] - step * energy
        send(2, residual + expand(own, old.basis), out.correction)
        wait(leaving)
        return

    keep = {}
    if kind == START:
        residual, local_residual = old.residual[...], old.local_after[...]
        energy_residual, partner_residual = energy, partner_traces()
        trace_residual = old.trace_after[...]
    else:
        if kind == FIRST:
            curvature, descent = dots[0], dots[1]
            direction, image, energy_image = old.correction[...], old.after[...], energy
            local_image, partner_image = old.local_after[...], partner_traces()
            trace_image = old.trace_after[...]
        else:
            curvature, descent, blend = update(dots, old.curvature)
            direction = old.correction[...] + blend * old.direction[...]
            image = old.after[...] + blend * old.image[...]
            energy_image = energy + blend * old.energy_image[...]
            local_image = old.local_after[...] + blend * old.local_image[...]
            partner_image = partner_traces() + blend * old.partner_image[...]
            trace_image = old.trace_after[...] + blend * old.trace_image[...]
        step = descent / curvature
        residual = old.residual[...] - step * image
        energy_residual = old.energy_residual[...] - step * energy_image
        out.solution[...] = step * direction + (0.0 if kind == FIRST else old.solution[...])
        keep.update(residual=residual, direction=direction, image=image, energy_image=energy_image)
        keep.update(curvature=jnp.broadcast_to(curvature, (loads, LANE)))
        local_residual = old.local_residual[...] - step * local_image
        partner_residual = old.partner_residual[...] - step * partner_image
        trace_residual = old.trace_residual[...] - step * trace_image
        keep.update(local_image=local_image, partner_image=partner_image, trace_image=trace_image)
    keep.update(energy_residual=energy_residual)

    own = energy_residual[:, LANE:]
    hi, lo = split(energy_residual[:, :LANE])
    pairs = jnp.concatenate(
        [jnp.concatenate([hi, hi], axis=1), jnp.concatenate([lo, lo], axis=1)], axis=0
    )
    other = jnp.dot(pairs, old.partner_basis[...], preferred_element_type=F32)
    partner = partner_residual + other[:loads] + other[loads:]
    trace = trace_residual + expand(own, old.face_basis)
    faces = old.faces
    live = jnp.concatenate([faces[g + 4 : g + 5, :] for g in range(4)], axis=1)
    jumps = jnp.where(live > 0, trace - partner, 0.0)
    correction = residual + expand(own, old.basis)
    keep.update(correction=correction)
    local = local_residual + expand(own, old.local_basis)
    after = correction + local

    dot = lambda a, b: jnp.sum(a * b, axis=1, keepdims=True)
    sums = [dot(correction, after) + dot(trace, jumps), dot(residual, correction)]
    if kind != START:
        sums += [dot(correction, image), dot(residual, direction)]
    coefs = coefficients(after, old.basis) + coefficients(jumps, old.face_basis)
    packed = pack(coefs, sums, (pos[0] * grid[1] + pos[1]) % 4)
    traces = []
    if kind != MIDDLE:
        tiles = tiles_of(after)
        traces = [pick_lanes(tiles, faces[g : g + 1, :]) for g in range(4)]
        traces = [t + j for t, j in zip(traces, tiles_of(jumps))]
        keep.update(trace_after=jnp.concatenate(traces, axis=1))
    write_slots(out.slots, packed, traces, sides)
    if kind == MIDDLE:
        after = jnp.concatenate(joined(after, jumps, old.named), axis=1)
    keep.update(after=after, jumps=jumps, trace_residual=trace_residual)
    keep.update(partner_residual=partner_residual, local_residual=local_residual)
    for k, v in keep.items():
        if hasattr(out, k):
            getattr(out, k)[...] = v


def exchange(slots):
    return lax.all_to_all(slots, AXES, 0, 0)


def pairs_of(count, odd):
    low = [(k, k + 1) for k in range(odd, count - 1, 2)]
    return low + [(b, a) for a, b in low]


def shards(
    grid, rhs, flex_tiles, flex_cols, stiff_tiles, stiff_cols, deflation, coarse_rows, face_rows, face_len
):
    loads, wide = rhs.shape
    defl, coarse = coarse_rows.shape
    blocks, per_row = flex_cols.shape
    count = grid[0] * grid[1]
    pos = jnp.stack([lax.axis_index("row"), lax.axis_index("col")]).astype(I32)
    whole = (loads, wide)
    slots = held((count, 3, 4, LANE))

    field, energy, traces = held(whole), held((loads, 256)), held((loads, 4 * LANE))

    slots_now, basis, faces, trace, rhs, deflation, coarse_rows = call(
        functools.partial(lead_kernel, grid),
        (
            slots,
            held((2 * defl, wide), BF16),
            held((8, LANE), I32),
            traces,
            field,
            held(deflation.shape),
            held(coarse_rows.shape),
        ),
        [SMEM] + [HBM] * 5,
        "lead",
        scratch=(pltpu.VMEM(face_len.shape, I32), pltpu.VMEM(face_rows.shape, I32), pltpu.SemaphoreType.DMA((5,))),
    )(pos, *in_hbm(rhs, deflation, coarse_rows, face_rows, face_len))
    received = exchange(slots_now)

    *copies, face_basis = call(
        copies_kernel,
        (jax.ShapeDtypeStruct((defl, coarse + LANE), F32),) * 4 + (held((2 * defl, 4 * LANE), BF16),),
        [VMEM, VMEM, VMEM],
        "copies",
    )(deflation, coarse_rows, faces)
    copies = [
        lax.ppermute(c, axis, pairs_of(n, odd))
        for c, (axis, n, odd) in zip(
            copies, (("row", grid[0], 0), ("row", grid[0], 1), ("col", grid[1], 0), ("col", grid[1], 1))
        )
    ]
    lists = in_hbm(flex_tiles, stiff_tiles, flex_cols.T, stiff_cols.T)

    def scratch(rows):
        return (
            (pltpu.VMEM((blocks, 2 * rows, LANE), BF16),) * 2
            + (pltpu.VMEM((blocks, rows, LANE), F32),)
            + (pltpu.VMEM(flex_tiles.shape, F32),) * 2
            + (pltpu.VMEM((flex_tiles.shape[0], 2 * LANE), BF16),) * 2
            + (pltpu.SMEM((per_row, blocks), I32),) * 2
            + (pltpu.SemaphoreType.DMA((4, 2)),)
        )

    local, local_basis, named, kept_tiles = call(
        first_local_kernel,
        (
            field,
            held((2 * defl, wide), BF16),
            held((blocks, LANE), I32),
            held((blocks // KEPT * per_row * LANE, 2 * LANE), BF16),
        ),
        [HBM] * 4 + [VMEM] * 3,
        "first_local",
        scratch(loads + defl),
    )(*lists, rhs, deflation, faces)
    weights, partner_basis = call(
        prepare_kernel,
        (held((3 * LANE, coarse), BF16), held((2 * LANE, 4 * LANE), BF16)),
        [VMEM] * 5,
        "prepare",
    )(coarse_rows, *copies)

    def apply_local(after, jumps):
        return call(local_kernel, (field, field), [HBM] * 4 + [VMEM] * 4, "local", scratch(loads))(
            *lists, after, jumps, named, kept_tiles
        )

    state = dict(
        pos=pos,
        received=received,
        weights=weights,
        basis=basis,
        local_basis=local_basis,
        partner_basis=partner_basis,
        faces=faces,
        face_basis=face_basis,
        named=named,
        residual=rhs,
        trace_after=trace,
        local_after=local,
        local_residual=local,
    )
    result = jax.ShapeDtypeStruct(whole, F32)

    def step(kind, **outs):
        last = kind == LAST
        done = call(
            functools.partial(step_kernel, grid, kind, tuple(state), tuple(outs)),
            tuple(outs.values()),
            [SMEM] + [VMEM] * (len(state) - 1),
            f"step{kind}",
            (pltpu.VMEM(whole, F32),) * 3 + (pltpu.SemaphoreType.DMA((3,)),) if last else (),
            (HBM,) * 3 if last else None,
        )(*state.values())
        state.update(zip(outs, done))

    step(
        START, slots=slots, correction=field, after=field, jumps=traces, energy_residual=energy,
        partner_residual=traces, trace_after=traces, trace_residual=traces,
    )
    for iteration in range(ITERS):
        state.update(received=exchange(state.pop("slots")))
        if iteration + 1 < ITERS:
            pair = apply_local(state["after"], state.pop("jumps"))
            state.update(zip(("after", "local_after"), pair))
        kept = dict(
            solution=field, residual=field, correction=field, direction=field, image=field, after=field,
            jumps=traces, energy_residual=energy, energy_image=energy, curvature=held((loads, LANE)), slots=slots,
        )
        more = dict(
            partner_residual=traces, local_residual=field, partner_image=traces, local_image=field,
            trace_residual=traces, trace_image=traces, trace_after=traces,
        )
        if iteration + 1 == ITERS:
            step(LAST, solution=result, residual=result, correction=result)
        elif iteration == 0 and ITERS > 2:
            step(FIRST, **kept, **more)
        else:
            kept.update(slots=held((count, 1, 4, LANE)))
            kept.pop("jumps")
            step(MIDDLE, **kept)
    return state["solution"], state["residual"], state["correction"]


def solution(mesh):
    grid = (mesh.shape["row"], mesh.shape["col"])
    return jax.shard_map(
        functools.partial(shards, grid),
        mesh=mesh,
        in_specs=(
            P("row", "col"),
            P("row", "col"),
            P("row", "col"),
            P("row", "col"),
            P("row", "col"),
            P("row", "col"),
            P(("row", "col"), None),
            P("row", "col"),
            P("row", "col"),
        ),
        out_specs=(P("row", "col"), P("row", "col"), P("row", "col")),
        check_vma=False,
    )
```
